256 devices in a mesh: gx: 8 (over y, core), gy: 16 (over x_lo, z), gz: 2 (over x_hi).
Axes of the slice: x: 4 (x_hi: 2, x_lo: 2; x = x_hi * 2 + x_lo), y: 4, z: 8, core: 2. Of those that a mesh axis runs over, the one named last changes fastest.
Arguments:
- field: float32 [16, 64, 8, 128], P('gx', 'gy', 'gz'), may hold values from -6 to 6
- parity_mask: int32 [16, 64, 8, 128], P('gx', 'gy', 'gz'), may hold values 0 or 1
- kernel_one: bfloat16 [16, 1, 3, 3, 3, 3], replicated, may hold values from -0.625 to 0.625
- bias_one: float32 [16], replicated, may hold values from -3 to 3
- kernel_two: bfloat16 [16, 16, 3, 3, 3, 3], replicated, may hold values from -0.15625 to 0.15625
- bias_two: float32 [16], replicated, may hold values from -3 to 3
- kernel_three: bfloat16 [2, 16, 3, 3, 3, 3], replicated, may hold values from -0.15625 to 0.15625
- bias_three: float32 [2], replicated, may hold values from -3 to 3
Outputs:
- flowed: float32 [16, 64, 8, 128], P('gx', 'gy', 'gz')
- field_grad: float32 [16, 64, 8, 128], P('gx', 'gy', 'gz')
- grad_kernel_one: float32 [16, 1, 3, 3, 3, 3], replicated
- grad_bias_one: float32 [16], replicated
- grad_kernel_two: float32 [16, 16, 3, 3, 3, 3], replicated
- grad_bias_two: float32 [16], replicated
- grad_kernel_three: float32 [2, 16, 3, 3, 3, 3], replicated
- grad_bias_three: float32 [2], replicated
The draws below stay inside these ranges and needn't reach their ends.
Inputs may be any that keep to these rules, and one draw needn't show every extreme that they name: parity_mask holds only 0 and 1.
All inputs are finite; a program needn't handle non-finite values. No bound on the sum of `parity_mask` on one device may be relied on, other than what follows from the above.
Results may differ from the reference program's by a relative error of at most 0.0073.
Values may be sent and summed in bfloat16 or wider, within the bound.
No kernel may reach another device: no remote copies, remote signals or barrier semaphores. Data moves between devices by JAX's collectives and lax.ppermute only.
A program may use at most 192 MiB of HBM per device.

```python
import jax
import jax.numpy as jnp
from jax import lax

CHANNELS = 16
TIME = 128
EXTENT_X = 16
EXTENT_Y = 64
EXTENT_Z = 8


def set_ends(array, rng, smallest, high):
    longest = array.shape.index(max(array.shape))
    spots = []
    for shift in (0, 1):
        where = [jax.random.randint(jax.random.fold_in(rng, axis), (), 0, length) for axis, length in enumerate(array.shape)]
        where[longest] = (where[longest] + shift) % array.shape[longest]
        spots.append(tuple(where))
    return array.at[spots[0]].set(smallest).at[spots[1]].set(high)


def level_of(rng, dims, split, smallest, high):
    def one(position, blocks):
        steps = jax.random.uniform(jax.random.fold_in(jax.random.fold_in(rng, 6), position), (blocks,), jnp.float32, smallest / len(split), high / len(split))
        return jnp.repeat(jnp.exp(steps), dims[position] // blocks).reshape((-1,) + (1,) * (len(dims) - position - 1))

    level = one(*split[0])
    for cut in split[1:]:
        level = level * one(*cut)
    return level


def bell_draw(rng, dims, deviation, bound, pieces=(), dtype=jnp.bfloat16):
    drawn = deviation * jax.random.normal(rng, dims, jnp.float32)
    if pieces:
        drawn = drawn * level_of(rng, dims, pieces, -0.22, 0.18)
    return jnp.clip(drawn, -bound, bound).astype(dtype)


def setup_inputs(seed: int = 0) -> dict:
    key_list = jax.random.split(jax.random.key(seed), 9)
    field = bell_draw(key_list[0], (EXTENT_X, EXTENT_Y, EXTENT_Z, TIME), 1.0, 6.0, ((0, 8), (1, 16), (2, 2)), jnp.float32)
    parity_mask = set_ends((jax.random.randint(key_list[1], (EXTENT_X, EXTENT_Y, EXTENT_Z, TIME), 0, 2) < 1).astype(jnp.int32), jax.random.fold_in(key_list[1], 1), 0, 1)
    kernel_one = bell_draw(key_list[2], (CHANNELS, 1, 3, 3, 3, 3), 81 ** -0.5, 0.625)
    bias_one = bell_draw(key_list[3], (CHANNELS,), 0.5, 3.0, (), jnp.float32)
    kernel_two = bell_draw(key_list[4], (CHANNELS, CHANNELS, 3, 3, 3, 3), (CHANNELS * 81) ** -0.5, 0.15625)
    bias_two = bell_draw(key_list[5], (CHANNELS,), 0.5, 3.0, (), jnp.float32)
    kernel_three = bell_draw(key_list[6], (2, CHANNELS, 3, 3, 3, 3), (CHANNELS * 81) ** -0.5, 0.15625)
    bias_three = bell_draw(key_list[7], (2,), 0.5, 3.0, (), jnp.float32)
    return dict(field=field, parity_mask=parity_mask, kernel_one=kernel_one, bias_one=bias_one, kernel_two=kernel_two, bias_two=bias_two, kernel_three=kernel_three, bias_three=bias_three)


hopping = 0.25
quartic = 0.05
layout_spec = lax.ConvDimensionNumbers((0, 1, 2, 3, 4, 5), (0, 1, 2, 3, 4, 5), (0, 1, 2, 3, 4, 5))

def wrap_pad(values):
    return jnp.pad(values, [(0, 0), (1, 1), (1, 1), (1, 1), (1, 1)], mode='wrap')

def correlate(padded, kernel):
    return lax.conv_general_dilated(padded[None], kernel, (1, 1, 1, 1), 'VALID', dimension_numbers=layout_spec, preferred_element_type=jnp.float32)[0]

def flip_kernel(kernel):
    return jnp.flip(kernel, axis=(2, 3, 4, 5)).transpose((1, 0, 2, 3, 4, 5))

def kernel_grad(padded, cotangent):
    result = lax.conv_general_dilated(padded[:, None], cotangent[:, None], (1, 1, 1, 1), 'VALID', dimension_numbers=layout_spec, preferred_element_type=jnp.float32)
    return result.transpose((1, 0, 2, 3, 4, 5))

def expand(bias):
    return bias[:, None, None, None, None]

def reference(field, parity_mask, kernel_one, bias_one, kernel_two, bias_two, kernel_three, bias_three):
    frozen_share = parity_mask.astype(jnp.float32)
    active_share = 1.0 - frozen_share
    frozen = (frozen_share * field).astype(jnp.bfloat16)[None]
    frozen_pad = wrap_pad(frozen)
    first_act = jnp.tanh(correlate(frozen_pad, kernel_one) + expand(bias_one)).astype(jnp.bfloat16)
    first_pad = wrap_pad(first_act)
    second_act = jnp.tanh(correlate(first_pad, kernel_two) + expand(bias_two)).astype(jnp.bfloat16)
    second_pad = wrap_pad(second_act)
    third_pre = correlate(second_pad, kernel_three) + expand(bias_three)
    scale_log = jnp.tanh(third_pre[0])
    growth = jnp.exp(scale_log)
    flowed = frozen_share * field + active_share * (field * growth + third_pre[1])
    neighbours = jnp.zeros_like(flowed)
    for axis_number in range(4):
        neighbours = neighbours + jnp.roll(flowed, 1, axis=axis_number) + jnp.roll(flowed, -1, axis=axis_number)
    force = -2.0 * hopping * neighbours + 2.0 * (1.0 - 2.0 * quartic) * flowed + 4.0 * quartic * flowed ** 3
    direct = force * (frozen_share + active_share * growth)
    scale_grad = active_share * (force * field * growth - 1.0) * (1.0 - scale_log * scale_log)
    third_cot = jnp.stack([scale_grad, active_share * force]).astype(jnp.bfloat16)
    second_float = second_act.astype(jnp.float32)
    second_cot = (correlate(wrap_pad(third_cot), flip_kernel(kernel_three)) * (1.0 - second_float * second_float)).astype(jnp.bfloat16)
    first_float = first_act.astype(jnp.float32)
    first_cot = (correlate(wrap_pad(second_cot), flip_kernel(kernel_two)) * (1.0 - first_float * first_float)).astype(jnp.bfloat16)
    field_grad = direct + frozen_share * correlate(wrap_pad(first_cot), flip_kernel(kernel_one))[0]
    volume = 1.0 * field.size
    grad_kernel_one = kernel_grad(frozen_pad, first_cot) / volume
    grad_kernel_two = kernel_grad(first_pad, second_cot) / volume
    grad_kernel_three = kernel_grad(second_pad, third_cot) / volume
    grad_bias_one = lax.optimization_barrier(jnp.sum(first_cot.astype(jnp.float32), axis=(1, 2, 3, 4))) / volume
    grad_bias_two = lax.optimization_barrier(jnp.sum(second_cot.astype(jnp.float32), axis=(1, 2, 3, 4))) / volume
    grad_bias_three = lax.optimization_barrier(jnp.sum(third_cot.astype(jnp.float32), axis=(1, 2, 3, 4))) / volume
    return (flowed, field_grad, grad_kernel_one, grad_bias_one, grad_kernel_two, grad_bias_two, grad_kernel_three, grad_bias_three)
```

```python
import functools

import jax
import jax.numpy as jnp
import numpy as np
from jax import lax
from jax.experimental import pallas as pl
from jax.experimental.pallas import tpu as pltpu
from jax.sharding import Mesh
from jax.sharding import PartitionSpec as P

F32 = jnp.float32
BF16 = jnp.bfloat16
GROUP = ("gz", "gx", "gyl")
VMEM_SPEC = pl.BlockSpec(memory_space=pltpu.VMEM)
VOLUME = 1048576.0


def lane_permutation():
    matrix = np.zeros((512, 512), np.float32)
    for gz in range(2):
        for gx in range(8):
            for x in range(2):
                for y in range(4):
                    for z in range(4):
                        source = (gz * 8 + gx) * 32 + x * 16 + y * 4 + z
                        target = y * 128 + (15 - gx * 2 - x) * 8 + gz * 4 + z
                        matrix[source, target] = 1.0
    return matrix


def pack_kernel(field_ref, mask_ref, out_ref, window):
    both = jnp.concatenate([field_ref[...], mask_ref[...].astype(F32)], axis=0)
    rolled = jnp.concatenate([pltpu.roll(both, 7, 1), pltpu.roll(both, 119, 1)], axis=0)
    turned = rolled.T
    window[0:128, :] = turned
    window[128:144, :] = turned[0:16, :]
    for slot in range(32):
        out_ref[slot] = window[4 * slot : 4 * slot + 16, :]


def weights_kernel(k2_ref, k2t_ref, k3_ref, k1_ref, w2_ref, w2t_ref, w3_ref, w1t_ref):
    lane = lax.broadcasted_iota(jnp.int32, (16, 128), 1)
    zero = jnp.zeros((16, 128), F32)

    def pick(parts, zone, wanted):
        total = zero
        for part, where in zip(parts, wanted):
            total = jnp.where(zone == where, part, total)
        return total.astype(BF16)

    def body(off, carry):
        k2 = [k2_ref[off * 3 + ez].astype(F32) for ez in range(3)]
        k2t = [k2t_ref[off * 3 + ez].astype(F32) for ez in range(3)]
        k3 = [[k3_ref[off * 3 + ez, o].astype(F32) for ez in range(3)] for o in range(2)]
        k1 = [k1_ref[off * 3 + ez].astype(F32) for ez in range(3)]
        for zin in range(8):
            forward = [(zin - ez + 1) % 8 for ez in range(3)]
            backward = [(zin + ez - 1) % 8 for ez in range(3)]
            rows = pl.ds(pl.multiple_of(off * 128 + zin * 16, 16), 16)
            w2_ref[rows, :] = pick(k2, lane // 16, forward)
            w2t_ref[rows, :] = pick(k2t, lane // 16, backward)
            w3_ref[rows, 0:128] = pick(k3[0], lane % 8, forward)
            w3_ref[rows, 128:256] = pick(k3[1], lane % 8, forward)
            w1t_ref[rows, :] = pick(k1, lane % 8, backward)
        return carry

    lax.fori_loop(0, 27, body, 0)


def split_dot(values, matrix, parts, transposed=False):
    dims = (((1,), (1 if transposed else 0,)), ((), ()))
    total = None
    rest = values
    for _ in range(parts):
        head = rest.astype(BF16)
        rest = rest - head.astype(F32)
        term = lax.dot_general(head, matrix, dims, preferred_element_type=F32)
        total = term if total is None else total + term
    return total


def spread(rows_value, base):
    count = rows_value.shape[0]
    turned = pltpu.roll(rows_value, 16 + base, 1)
    wide = jnp.broadcast_to(turned[:, None, :], (count, 16, 128))
    return pltpu.roll(wide, 0, 2, stride=8, stride_axis=1)


def spread_rows(rows_value):
    count = rows_value.shape[0]
    lane = lax.broadcasted_iota(jnp.int32, (count - 2, 16, 128), 2)
    low = spread(rows_value[0 : count - 2], 0)
    mid = spread(rows_value[1 : count - 1], 24)
    high = spread(rows_value[2:count], 48)
    return jnp.where(lane < 24, low, jnp.where(lane < 48, mid, high))


def store_shifted(ref, time, values):
    ref[time, :, :, 0:128] = pltpu.roll(values, 1, 1).astype(BF16)
    ref[time, :, :, 128:256] = values.astype(BF16)
    ref[time, :, :, 256:384] = pltpu.roll(values, 15, 1).astype(BF16)


def nine_dot(ref, time, rows, w_ref):
    total = None
    for first in range(3):
        for second in range(3):
            block = ref[time + first, second : second + rows].reshape(rows * 16, 384)
            at = (first * 3 + second) * 384
            term = jnp.dot(block, w_ref[at : at + 384, :], preferred_element_type=F32)
            total = term if total is None else total + term
    return total


def diagonal_sum(values, rows):
    lane = 15 - lax.broadcasted_iota(jnp.int32, (rows, 16, 128), 2) // 8
    site = lax.broadcasted_iota(jnp.int32, (rows, 16, 128), 1)
    return jnp.sum(jnp.where(lane == site, values.reshape(rows, 16, 128), 0.0), axis=1)


def fold_group(values):
    lane = lax.broadcasted_iota(jnp.int32, values.shape, 1)
    for step in (1, 2, 4):
        down = pltpu.roll(values, 128 - step, 1)
        up = pltpu.roll(values, step, 1)
        values = values + jnp.where((lane // step) % 2 == 0, down, up)
    return values


def main_kernel(
    low_ref, own_ref, high_ref, perm_ref, w1_ref, w3t_ref, w2_ref, w2t_ref, w3_ref, w1t_ref, bias_ref,
    out_ref,
    gather_f, gather_m, dense_f, dense_m, frozen_x, act1, act2, pre0, pre1, flow, scale_c, shift_c, direct,
    third_x, cot2, cot1, own_out, rows_out,
):
    for block, ref in enumerate((low_ref, own_ref, high_ref)):
        for source in range(32):
            spot, half = source // 2, source % 2
            lanes = slice(spot * 32, spot * 32 + 32)
            piece = ref[source]
            gather_f[block * 2 + half, 0:16, lanes] = piece[:, 0:32]
            gather_m[block * 2 + half, 0:16, lanes] = piece[:, 32:64]
            gather_f[block * 2 + half, 16:24, lanes] = piece[0:8, 64:96]
            gather_m[block * 2 + half, 16:24, lanes] = piece[0:8, 96:128]
    perm = perm_ref[...]
    sorted_f = split_dot(gather_f[...].reshape(144, 512), perm, 3)
    sorted_m = split_dot(gather_m[...].reshape(144, 512), perm, 1)
    for block in range(6):
        for y in range(4):
            lanes = slice(y * 128, y * 128 + 128)
            rows = pl.ds(block * 4 + y, 18, stride=24)
            dense_f[rows, :] = sorted_f[block * 24 : block * 24 + 18, lanes]
            dense_m[rows, :] = sorted_m[block * 24 : block * 24 + 18, lanes]

    def spread_frozen(time, carry):
        rows = pl.ds(pl.multiple_of(time * 24, 8), 24)
        frozen = (dense_f[rows, :] * dense_m[rows, :]).astype(BF16).astype(F32)
        frozen_x[time] = spread_rows(frozen[1:23]).astype(BF16)
        return carry

    lax.fori_loop(0, 18, spread_frozen, 0)

    def first_layer(time, carry):
        total = bias_ref[0:1, :]
        for first in range(3):
            block = frozen_x[time + first].reshape(320, 128)
            total = total + jnp.dot(
                block, w1_ref[first * 128 : first * 128 + 128, :], preferred_element_type=F32
            )
        store_shifted(act1, time, jnp.tanh(total).reshape(20, 16, 128))
        return carry

    lax.fori_loop(0, 16, first_layer, 0)

    def second_layer(time, carry):
        total = nine_dot(act1, time, 18, w2_ref) + bias_ref[1:2, :]
        store_shifted(act2, time, jnp.tanh(total).reshape(18, 16, 128))
        return carry

    lax.fori_loop(0, 14, second_layer, 0)

    def third_layer(time, carry):
        total = nine_dot(act2, time, 16, w3_ref)
        pre0[time] = diagonal_sum(total[:, 0:128], 16) + bias_ref[2:3, :]
        pre1[time] = diagonal_sum(total[:, 128:256], 16) + bias_ref[3:4, :]
        return carry

    lax.fori_loop(0, 12, third_layer, 0)

    def transform(time, carry):
        rows = pl.ds(pl.multiple_of((time + 3) * 24, 8), 24)
        field = dense_f[rows, :][4:20]
        share = dense_m[rows, :][4:20]
        growth = jnp.exp(jnp.tanh(pre0[time]))
        flow[time] = share * field + (1.0 - share) * (field * growth + pre1[time])
        return carry

    lax.fori_loop(0, 12, transform, 0)

    def force_step(time, carry):
        rows = pl.ds(pl.multiple_of((time + 4) * 24, 8), 24)
        field = dense_f[rows, :][5:19]
        share = dense_m[rows, :][5:19]
        here = flow[time + 1]
        lane = lax.broadcasted_iota(jnp.int32, (16, 128), 1) % 8
        around = flow[time] + flow[time + 2] + pltpu.roll(here, 8, 1) + pltpu.roll(here, 120, 1)
        around = around + jnp.where(lane == 0, pltpu.roll(here, 121, 1), pltpu.roll(here, 1, 1))
        around = around + jnp.where(lane == 7, pltpu.roll(here, 7, 1), pltpu.roll(here, 127, 1))
        around = around[1:15] + here[0:14] + here[2:16]
        mid = here[1:15]
        force = -0.5 * around + 1.8 * mid + 0.2 * mid * mid * mid
        scale = jnp.tanh(pre0[time + 1][1:15])
        growth = jnp.exp(scale)
        active = 1.0 - share
        scale_c[time] = (active * (force * field * growth - 1.0) * (1.0 - scale * scale)).astype(BF16).astype(F32)
        shift_c[time] = (active * force).astype(BF16).astype(F32)
        direct[time] = force * (share + active * growth)
        third_x[time, :, :, 0:128] = spread_rows(scale_c[time]).astype(BF16)
        third_x[time, :, :, 128:256] = spread_rows(shift_c[time]).astype(BF16)
        return carry

    lax.fori_loop(0, 10, force_step, 0)

    def second_cot(time, carry):
        total = None
        for first in range(3):
            block = third_x[time + first].reshape(192, 256)
            term = jnp.dot(
                block, w3t_ref[first * 256 : first * 256 + 256, :], preferred_element_type=F32
            )
            total = term if total is None else total + term
        act = act2[time + 3, 3:15, :, 128:256].astype(F32)
        values = total.reshape(12, 16, 128) * (1.0 - act * act)
        store_shifted(cot2, time, values)
        return carry

    lax.fori_loop(0, 8, second_cot, 0)

    def first_cot(time, carry):
        total = nine_dot(cot2, time, 10, w2t_ref)
        act = act1[time + 5, 5:15, :, 128:256].astype(F32)
        values = total.reshape(10, 16, 128) * (1.0 - act * act)
        store_shifted(cot1, time, values)
        return carry

    lax.fori_loop(0, 6, first_cot, 0)

    for time in range(4):
        total = diagonal_sum(nine_dot(cot1, time, 8, w1t_ref), 8)
        own_out[time * 8 : time * 8 + 8, :] = flow[time + 4][4:12]
        own_out[32 + time * 8 : 40 + time * 8, :] = (
            direct[time + 3][3:11] + dense_m[(time + 7) * 24 + 8 : (time + 7) * 24 + 16, :] * total
        )

    for kind in range(2):
        for half in range(2):
            for y in range(4):
                rows_out[(kind * 2 + half) * 4 : (kind * 2 + half) * 4 + 4, y * 128 : y * 128 + 128] = own_out[
                    pl.ds(kind * 32 + half * 4 + y, 4, stride=8), :
                ]
    ordered = split_dot(rows_out[...], perm, 3, transposed=True)
    for target in range(32):
        spot, half = target // 2, target % 2
        lanes = slice(spot * 32, spot * 32 + 32)
        out_ref[target, 8:12, 0:32] = ordered[half * 4 : half * 4 + 4, lanes]
        out_ref[target, 8:12, 32:64] = ordered[8 + half * 4 : 12 + half * 4, lanes]

    def put(block, values):
        out_ref[2 * block, 0:8, :] = values[0:8]
        out_ref[2 * block + 1, 0:8, :] = values[8:16]

    own2 = cot2[2:6, 2:10, :, 128:256].reshape(512, 128).astype(F32)
    own1 = cot1[1:5, 1:9, :, 128:256].reshape(512, 128).astype(F32)
    own_a = act2[5:9, 5:13, :, 128:256].reshape(512, 128).astype(F32)
    turn2 = own2.T.astype(BF16)
    turn1 = own1.T.astype(BF16)
    turn_a = own_a.T.astype(BF16)
    zone = lax.broadcasted_iota(jnp.int32, (16, 128), 1)

    def lane_sum(values, lanes_zone, shift):
        total = jnp.zeros((16, 128), F32)
        for z in range(8):
            total = total + jnp.where(lanes_zone == (z + shift) % 8, values[z * 16 : z * 16 + 16], 0.0)
        return total

    packed = [None] * 11
    for first in range(3):
        for second in range(3):
            block = act1[5 + first : 9 + first, 5 + second : 13 + second].reshape(512, 384)
            product = jnp.dot(turn2, block, preferred_element_type=F32)
            for third in range(3):
                for ez in range(3):
                    number = ((first * 3 + second) * 3 + third) * 3 + ez
                    part = lane_sum(product[:, third * 128 : third * 128 + 128], zone // 16, ez - 1)
                    for step in (64, 32, 16):
                        part = part + pltpu.roll(part, step, 1)
                    old = packed[number // 8]
                    packed[number // 8] = (
                        part if old is None else jnp.where(zone // 16 == number % 8, part, old)
                    )
    for number in range(11):
        put(number, packed[number])

    extra = jnp.zeros((16, 128), F32)
    for first in range(3):
        block = third_x[2 + first : 6 + first, 2:10].reshape(512, 256)
        product = jnp.dot(turn_a, block, preferred_element_type=F32)
        total = jnp.zeros((16, 128), F32)
        for o in range(2):
            for ez in range(3):
                part = fold_group(lane_sum(product[:, o * 128 : o * 128 + 128], zone % 8, 1 - ez))
                total = jnp.where(zone % 8 == o * 3 + ez, part, total)
        block = frozen_x[6 + first : 10 + first, 6:14].reshape(512, 128)
        product = jnp.dot(turn1, block, preferred_element_type=F32)
        for ez in range(3):
            part = fold_group(lane_sum(product, zone % 8, ez - 1))
            if ez < 2:
                total = jnp.where(zone % 8 == 6 + ez, part, total)
            else:
                extra = jnp.where(zone % 8 == first, part, extra)
        put(11 + first, total)
    put(14, extra)
    sums = [
        jnp.sum(own1, axis=0, keepdims=True),
        jnp.sum(own2, axis=0, keepdims=True),
        jnp.sum(jnp.sum(scale_c[3:7], axis=0)[3:11], axis=0, keepdims=True),
        jnp.sum(jnp.sum(shift_c[3:7], axis=0)[3:11], axis=0, keepdims=True),
    ]
    site = lax.broadcasted_iota(jnp.int32, (16, 128), 0)
    total = jnp.zeros((16, 128), F32)
    for row, value in enumerate(sums):
        total = jnp.where(site == row, jnp.broadcast_to(value, (16, 128)), total)
    put(15, total)


def unpack_kernel(in_ref, flowed_ref, grad_ref, share_ref, window):
    total = in_ref[0, 0:8, :]
    for source in range(1, 32):
        total = total + in_ref[source, 0:8, :]
    for target in range(8):
        share_ref[target] = total
    for source in range(32):
        window[4 * source : 4 * source + 4, :] = in_ref[source, 8:12, :]
    turned = window[...].T
    flowed_ref[...] = turned[0:32]
    grad_ref[...] = turned[32:64]


def ring(count, step):
    return [(i, (i + step) % count) for i in range(count)]


def prepare_weights(kernel_one, kernel_two, kernel_three):
    circle = np.zeros((3, 8, 8), np.float32)
    for ez in range(3):
        for z in range(8):
            circle[ez, (z + ez - 1) % 8, z] = 1.0
    circle = jnp.asarray(circle, BF16)
    k1 = kernel_one[:, 0]
    w1 = jnp.einsum("oxyet,eab->tyxabo", k1[:, ::-1], circle).reshape(3, 72, 128)
    w1 = jnp.pad(w1, ((0, 0), (0, 56), (0, 0))).reshape(384, 128)
    k3f = kernel_three[:, :, :, ::-1, :, ::-1]
    w3t = jnp.einsum("cixyet,eba->tcyxabi", k3f, circle).reshape(6, 72, 128)
    w3t = jnp.pad(w3t, ((0, 0), (0, 56), (0, 0))).reshape(768, 128)
    k2a = kernel_two.transpose(5, 3, 2, 4, 1, 0).reshape(81, 16, 1, 16)
    k2a = jnp.broadcast_to(k2a, (81, 16, 8, 16)).reshape(81, 16, 128)
    k2f = kernel_two[:, :, ::-1, ::-1, :, ::-1]
    k2t = k2f.transpose(5, 3, 2, 4, 0, 1).reshape(81, 16, 1, 16)
    k2t = jnp.broadcast_to(k2t, (81, 16, 8, 16)).reshape(81, 16, 128)
    k3 = kernel_three.transpose(5, 3, 2, 4, 0, 1).reshape(81, 2, 16, 1)
    k3 = jnp.broadcast_to(k3, (81, 2, 16, 128))
    k1b = k1[:, ::-1, ::-1, :, ::-1].transpose(4, 2, 1, 3, 0).reshape(81, 16, 1)
    k1b = jnp.broadcast_to(k1b, (81, 16, 128))
    w2, w2t, w3, w1t = pl.pallas_call(
        weights_kernel,
        out_shape=[
            jax.ShapeDtypeStruct((3456, 128), BF16),
            jax.ShapeDtypeStruct((3456, 128), BF16),
            jax.ShapeDtypeStruct((3456, 256), BF16),
            jax.ShapeDtypeStruct((3456, 128), BF16),
        ],
        in_specs=[VMEM_SPEC] * 4,
        out_specs=[VMEM_SPEC] * 4,
        compiler_params=pltpu.CompilerParams(vmem_limit_bytes=20 * 2**20),
        cost_estimate=pl.CostEstimate(flops=10**6, bytes_accessed=8 * 10**6, transcendentals=0),
        name="weights",
    )(k2a, k2t, k3, k1b)
    return w1, w3t, w2, w2t, w3, w1t


def local(field, parity_mask, kernel_one, bias_one, kernel_two, bias_two, kernel_three, bias_three):
    packed = pl.pallas_call(
        pack_kernel,
        out_shape=jax.ShapeDtypeStruct((32, 16, 128), F32),
        in_specs=[VMEM_SPEC] * 2,
        out_specs=VMEM_SPEC,
        scratch_shapes=[pltpu.VMEM((144, 128), F32)],
        name="pack",
    )(field.reshape(32, 128), parity_mask.reshape(32, 128))
    own = lax.all_to_all(packed, GROUP, 0, 0)
    low = lax.ppermute(own, "gyh", ring(8, 1))
    high = lax.ppermute(own, "gyh", ring(8, -1))
    w1, w3t, w2, w2t, w3, w1t = prepare_weights(kernel_one, kernel_two, kernel_three)
    bias = jnp.stack(
        [
            jnp.tile(bias_one, 8),
            jnp.tile(bias_two, 8),
            jnp.broadcast_to(bias_three[0], (128,)),
            jnp.broadcast_to(bias_three[1], (128,)),
        ]
    )
    perm = jnp.asarray(lane_permutation(), BF16)
    result = pl.pallas_call(
        main_kernel,
        out_shape=jax.ShapeDtypeStruct((32, 16, 128), F32),
        in_specs=[VMEM_SPEC] * 11,
        out_specs=VMEM_SPEC,
        scratch_shapes=[
            pltpu.VMEM((6, 24, 512), F32),
            pltpu.VMEM((6, 24, 512), F32),
            pltpu.VMEM((432, 128), F32),
            pltpu.VMEM((432, 128), F32),
            pltpu.VMEM((18, 20, 16, 128), BF16),
            pltpu.VMEM((16, 20, 16, 384), BF16),
            pltpu.VMEM((14, 18, 16, 384), BF16),
            pltpu.VMEM((12, 16, 128), F32),
            pltpu.VMEM((12, 16, 128), F32),
            pltpu.VMEM((12, 16, 128), F32),
            pltpu.VMEM((10, 14, 128), F32),
            pltpu.VMEM((10, 14, 128), F32),
            pltpu.VMEM((10, 14, 128), F32),
            pltpu.VMEM((10, 12, 16, 256), BF16),
            pltpu.VMEM((8, 12, 16, 384), BF16),
            pltpu.VMEM((6, 10, 16, 384), BF16),
            pltpu.VMEM((64, 128), F32),
            pltpu.VMEM((16, 512), F32),
        ],
        compiler_params=pltpu.CompilerParams(vmem_limit_bytes=48 * 2**20),
        cost_estimate=pl.CostEstimate(flops=2 * 10**10, bytes_accessed=8 * 10**6, transcendentals=10**6),
        name="flow",
    )(low, own, high, perm, w1, w3t, w2, w2t, w3, w1t, bias)
    back = lax.all_to_all(result, GROUP, 0, 0)
    flowed, field_grad, share = pl.pallas_call(
        unpack_kernel,
        out_shape=[
            jax.ShapeDtypeStruct((32, 128), F32),
            jax.ShapeDtypeStruct((32, 128), F32),
            jax.ShapeDtypeStruct((8, 8, 128), F32),
        ],
        in_specs=[VMEM_SPEC],
        out_specs=[VMEM_SPEC] * 3,
        scratch_shapes=[pltpu.VMEM((128, 128), F32)],
        name="unpack",
    )(back)
    share = lax.all_to_all(share, "gyh", 0, 0)
    share = jnp.sum(share, axis=0) * (1.0 / VOLUME)
    total = lax.all_to_all(jnp.broadcast_to(share[None], (32, 8, 128)), GROUP, 0, 0).reshape(256, 128)
    grad_two = total[0:176].reshape(11, 16, 8, 16).transpose(0, 2, 1, 3).reshape(88, 16, 16)[:81]
    grad_kernel_two = grad_two.reshape(3, 3, 3, 3, 16, 16).transpose(4, 5, 2, 1, 3, 0)
    mixed = total[176:224].reshape(3, 16, 128)[:, :, :72].reshape(3, 16, 3, 3, 8)
    third = mixed[::-1, :, ::-1, :, 0:6].reshape(3, 16, 3, 3, 2, 3)
    grad_kernel_three = third.transpose(4, 1, 3, 2, 5, 0)
    last = total[224:240][:, :72].reshape(16, 3, 3, 8)[..., 0:3].transpose(3, 0, 1, 2)
    one = jnp.concatenate([mixed[..., 6:8], last[..., None]], axis=-1)
    grad_kernel_one = one[:, :, :, ::-1].transpose(1, 3, 2, 4, 0)[:, None]
    sums = total[240:244]
    grad_bias_one = jnp.sum(sums[0].reshape(8, 16), axis=0)
    grad_bias_two = jnp.sum(sums[1].reshape(8, 16), axis=0)
    grad_bias_three = jnp.sum(sums[2:4], axis=1)
    return (
        flowed.reshape(2, 4, 4, 128),
        field_grad.reshape(2, 4, 4, 128),
        grad_kernel_one,
        grad_bias_one,
        grad_kernel_two,
        grad_bias_two,
        grad_kernel_three,
        grad_bias_three,
    )


def solution(mesh):
    split = Mesh(mesh.devices.reshape(8, 8, 2, 2), ("gx", "gyh", "gyl", "gz"))
    block = P("gx", ("gyh", "gyl"), "gz", None)
    return jax.shard_map(
        local,
        mesh=split,
        in_specs=(block, block, P(), P(), P(), P(), P(), P()),
        out_specs=(block, block, P(), P(), P(), P(), P(), P()),
        check_vma=False,
    )
```

```python
import functools

import jax
import jax.numpy as jnp
import numpy as np
from jax import lax
from jax.experimental import pallas as pl
from jax.experimental.pallas import tpu as pltpu
from jax.sharding import Mesh
from jax.sharding import PartitionSpec as P

F32 = jnp.float32
BF16 = jnp.bfloat16
GROUP = ("gz", "gx", "gyl")
VMEM_SPEC = pl.BlockSpec(memory_space=pltpu.VMEM)
HBM_SPEC = pl.BlockSpec(memory_space=pltpu.HBM)
VOLUME = 1048576.0


def lane_permutation():
    matrix = np.zeros((512, 512), np.float32)
    for gz in range(2):
        for gx in range(8):
            for x in range(2):
                for y in range(4):
                    for z in range(4):
                        source = (gz * 8 + gx) * 32 + x * 16 + y * 4 + z
                        target = y * 128 + (gx * 2 + x) * 8 + gz * 4 + z
                        matrix[source, target] = 1.0
    return matrix


def split_kernel(field_ref, mask_ref, out_ref):
    field = field_ref[...]
    head = field.astype(BF16)
    out_ref[0:32, :] = head
    out_ref[32:64, :] = (field - head.astype(F32)).astype(BF16)
    out_ref[64:96, :] = mask_ref[...].astype(F32).astype(BF16)


def pack_kernel(low_ref, own_ref, high_ref, out_ref, window):
    empty = jnp.zeros((32, 128), F32)

    def turn(ref):
        both = ref[...].astype(F32)
        near = jnp.concatenate([pltpu.roll(both, 7, 1), empty], axis=0).T
        later = jnp.concatenate([empty, pltpu.roll(both, 119, 1)], axis=0).T
        return near, later

    low, low_later = turn(low_ref)
    own, own_later = turn(own_ref)
    high, high_later = turn(high_ref)
    lane = lax.broadcasted_iota(jnp.int32, (128, 128), 1)
    rows = [
        jnp.where(lane < 96, low, pltpu.roll(own, 96, 1)),
        jnp.where(lane < 64, pltpu.roll(own, 96, 1), pltpu.roll(high, 64, 1)),
        pltpu.roll(high, 64, 1),
        low_later,
        pltpu.roll(own_later, 2, 0),
        pltpu.roll(high_later, 4, 0),
    ]
    for number, value in enumerate(rows):
        window[number, 0:128, :] = value
        window[number, 128:144, :] = value[0:16, :]
    lane = lax.broadcasted_iota(jnp.int32, (16, 128), 1)
    row = lax.broadcasted_iota(jnp.int32, (16, 128), 0)
    for slot in range(32):
        here = slice(4 * slot, 4 * slot + 16)
        out_ref[slot, 0:16, :] = window[0, here, :].astype(BF16)
        out_ref[slot, 16:32, :] = window[1, here, :].astype(BF16)
        tail = jnp.where(row < 2, window[3, here, :], jnp.where(row < 4, window[4, here, :], window[5, here, :]))
        out_ref[slot, 32:48, :] = jnp.where(lane < 32, window[2, here, :], tail).astype(BF16)


def tile_dot(values):
    spot = lax.broadcasted_iota(jnp.int32, (16, 128), 0)
    lane = lax.broadcasted_iota(jnp.int32, (16, 128), 1)
    return jnp.dot(values, jnp.where(lane % 16 == spot, 1.0, 0.0).astype(BF16), preferred_element_type=F32)


def weights_kernel(
    k1_ref, k2_ref, k3_ref, b1_ref, b2_ref, b3_ref,
    w1_hbm, w3t_hbm, w2_hbm, w2t_hbm, w3_hbm, w1t_hbm, bias_hbm,
    w1_ref, w3t_ref, w2_ref, w2t_ref, w3_ref, w1t_ref, bias_ref, one, two, three, sems,
):
    def at(ex, ey, ez, et):
        return ((ex * 3 + ey) * 3 + ez) * 3 + et

    one[...] = tile_dot(k1_ref[...])
    two[...] = tile_dot(k2_ref[...])
    three[...] = tile_dot(k3_ref[...])
    zone = lax.broadcasted_iota(jnp.int32, (8, 128), 1) // 16
    spot = lax.broadcasted_iota(jnp.int32, (8, 128), 0)
    wide = lax.broadcasted_iota(jnp.int32, (16, 128), 1) // 16
    zeros = jnp.zeros((128, 128), BF16)

    def rows8(ref, base, ex, ey, et, ahead):
        total = jnp.zeros((8, 128), F32)
        for ez in range(3):
            value = jnp.broadcast_to(ref[base(at(ex, ey, ez, et)), :], (8, 128))
            total = jnp.where(zone == (spot + ahead * (ez - 1) + 8) % 8, value, total)
        return total

    def row_one(off):
        return slice(off, off + 1)

    def row_three(o):
        return lambda off: slice(off * 2 + o, off * 2 + o + 1)

    for et in range(3):
        w1_ref[et * 128 + 72 : et * 128 + 128, :] = jnp.zeros((56, 128), BF16)
        for ey in range(3):
            block = [rows8(one, row_one, 2 - turned, ey, et, -1) for turned in range(3)]
            w1_ref[et * 128 + ey * 24 : et * 128 + ey * 24 + 24, :] = jnp.concatenate(block, axis=0).astype(BF16)
        for o in range(2):
            base = (et * 2 + o) * 128
            w3t_ref[base + 72 : base + 128, :] = jnp.zeros((56, 128), BF16)
            for dy in range(3):
                block = [rows8(three, row_three(o), turned, 2 - dy, 2 - et, 1) for turned in range(3)]
                w3t_ref[base + dy * 24 : base + dy * 24 + 24, :] = jnp.concatenate(block, axis=0).astype(BF16)
        for ex in range(3):
            block = []
            for ey in range(3):
                for o in range(2):
                    block.append(rows8(three, row_three(o), ex, ey, et, 1))
            block.append(jnp.zeros((80, 128), F32))
            rows = slice((et * 3 + ex) * 128, (et * 3 + ex) * 128 + 128)
            w3_ref[rows, :] = jnp.concatenate(block, axis=0).T.astype(BF16)
            block = [rows8(one, row_one, 2 - ex, 2 - dy, 2 - et, -1) for dy in range(3)]
            block.append(jnp.zeros((104, 128), F32))
            w1t_ref[rows, :] = jnp.concatenate(block, axis=0).T.astype(BF16)
            for ey in range(3):
                parts = [two[at(ex, ey, ez, et) * 16 : at(ex, ey, ez, et) * 16 + 16, :] for ez in range(3)]
                block = []
                for z in range(8):
                    total = jnp.zeros((16, 128), F32)
                    for ez in range(3):
                        total = jnp.where(wide == (z + ez - 1) % 8, parts[ez], total)
                    block.append(total)
                block = jnp.concatenate(block, axis=0)
                turned = block.T.astype(BF16)
                block = block.astype(BF16)
                for member in range(2):
                    lanes = slice(member * 128, member * 128 + 128)
                    base = ((et * 4 + ey + member) * 3 + ex) * 128
                    w2_ref[base : base + 128, lanes] = turned
                    base = (((2 - et) * 4 + 2 - ey + member) * 3 + 2 - ex) * 128
                    w2t_ref[base : base + 128, lanes] = block
            for member in range(2):
                lanes = slice(member * 128, member * 128 + 128)
                base = ((et * 4 + 3 * (1 - member)) * 3 + ex) * 128
                w2_ref[base : base + 128, lanes] = zeros
                w2t_ref[base : base + 128, lanes] = zeros
    bias_ref[0:1, :] = jnp.concatenate([b1_ref[...]] * 8, axis=1)
    bias_ref[1:2, :] = jnp.concatenate([b2_ref[...]] * 8, axis=1)
    bias_ref[2:3, :] = jnp.broadcast_to(b3_ref[0:1, 0:1], (1, 128))
    bias_ref[3:4, :] = jnp.broadcast_to(b3_ref[0:1, 1:2], (1, 128))
    copies = []
    for number, (source, target) in enumerate(
        (
            (w1_ref, w1_hbm),
            (w3t_ref, w3t_hbm),
            (w2_ref, w2_hbm),
            (w2t_ref, w2t_hbm),
            (w3_ref, w3_hbm),
            (w1t_ref, w1t_hbm),
            (bias_ref, bias_hbm),
        )
    ):
        copies.append(pltpu.make_async_copy(source, target, sems.at[number]))
        copies[-1].start()
    for copy in copies:
        copy.wait()


def split_dot(values, matrix, parts, transposed=False):
    dims = (((1,), (1 if transposed else 0,)), ((), ()))
    total = None
    rest = values
    for _ in range(parts):
        head = rest.astype(BF16)
        rest = rest - head.astype(F32)
        term = lax.dot_general(head, matrix, dims, preferred_element_type=F32)
        total = term if total is None else total + term
    return total


def reverse_matrix():
    source = lax.broadcasted_iota(jnp.int32, (128, 128), 0)
    target = lax.broadcasted_iota(jnp.int32, (128, 128), 1)
    return jnp.where(source == (15 - target // 8) * 8 + target % 8, 1.0, 0.0).astype(BF16)


def spread_rows(values):
    count = values.shape[0] - 2
    site = lax.broadcasted_iota(jnp.int32, (count, 16, 128), 1)
    lane = (lax.broadcasted_iota(jnp.int32, (count, 16, 128), 2) + 8 * site) % 128
    pieces = []
    for second in range(3):
        turned = pltpu.roll(values, 16 + 24 * second, 1)[second : second + count]
        pieces.append(jnp.broadcast_to(turned[:, None, :], (count, 16, 128)))
    wide = jnp.where(lane < 24, pieces[0], jnp.where(lane < 48, pieces[1], pieces[2]))
    return pltpu.roll(wide, 0, 2, stride=8, stride_axis=1)


def gather_rows(values, place):
    count = values.shape[0]
    site = lax.broadcasted_iota(jnp.int32, (count, 16, 128), 1)
    lane = lax.broadcasted_iota(jnp.int32, (count, 16, 128), 2) // 8
    moved = pltpu.roll(values, 0, 2, stride=8, stride_axis=1)
    results = []
    for spot in range(place):
        total = jnp.sum(jnp.where(lane == (site + spot) % 16, moved, 0.0), axis=1)
        results.append(total if spot == 0 else pltpu.roll(total, 128 - 8 * spot, 1))
    return results


def shifted(values):
    return (
        pltpu.roll(values, 1, 1).astype(BF16),
        values.astype(BF16),
        pltpu.roll(values, 15, 1).astype(BF16),
    )


def pair_dot(ref, time, steps, pairs, w_ref):
    total = None
    for first in range(3):
        for block in range(4):
            rows = ref[pl.ds(time + first, steps), block // 2 : block // 2 + pairs, block % 2]
            rows = rows.reshape(steps * pairs * 16, 384)
            at = (first * 4 + block) * 384
            term = jnp.dot(rows, w_ref[at : at + 384, :], preferred_element_type=F32)
            total = term if total is None else total + term
    return total


def time_dot(ref, time, rows, w_ref):
    total = None
    for first in range(3):
        block = ref[time + first].reshape(rows, 384)
        term = jnp.dot(block, w_ref[first * 384 : first * 384 + 384, :], preferred_element_type=F32)
        total = term if total is None else total + term
    return total


def fold_group(values):
    lane = lax.broadcasted_iota(jnp.int32, values.shape, 1)
    for step in (1, 2, 4):
        down = pltpu.roll(values, 128 - step, 1)
        up = pltpu.roll(values, step, 1)
        values = values + jnp.where((lane // step) % 2 == 0, down, up)
    return values


def main_kernel(
    in_ref, perm_hbm, w1_hbm, w3t_hbm, w2_hbm, w2t_hbm, w3_hbm, bias_hbm,
    out_ref, cot1_hbm, held,
    gather, dense_f, dense_m, dense_z, frozen, frozen_x, act1, act2, pre0, pre1, flow, scale_c, shift_c,
    direct, third_x, cot2, cot1, perm_ref, w1_ref, w3t_ref, w2_ref, w2t_ref, w3_ref, bias_ref, sems,
):
    copies = {}
    for number, (name, source, target) in enumerate(
        (
            ("perm", perm_hbm, perm_ref),
            ("w1", w1_hbm, w1_ref),
            ("bias", bias_hbm, bias_ref),
            ("w2", w2_hbm, w2_ref),
            ("w3", w3_hbm, w3_ref),
            ("w3t", w3t_hbm, w3t_ref),
            ("w2t", w2t_hbm, w2t_ref),
        )
    ):
        copies[name] = pltpu.make_async_copy(source, target, sems.at[number])
        copies[name].start()

    def repeat(count, body):
        for step in range(count):
            body(step)

    for source in range(32):
        spot, half = source // 2, source % 2
        lanes = slice(spot * 32, spot * 32 + 32)
        tiles = [in_ref[source, 16 * tile : 16 * tile + 16, :].astype(F32) for tile in range(3)]
        for block in range(3):
            for kind in range(3):
                piece = block * 3 + kind
                at = piece % 4 * 32
                gather[kind * 6 + block * 2 + half, 0:16, lanes] = tiles[piece // 4][:, at : at + 32]
                at = 32 + 32 * kind
                gather[kind * 6 + block * 2 + half, 16:18, lanes] = tiles[2][2 * block : 2 * block + 2, at : at + 32]
    copies["perm"].wait()
    ordered = jnp.dot(
        gather[...].reshape(432, 512).astype(BF16), perm_ref[...], preferred_element_type=F32
    )
    for block in range(6):
        head = ordered[block * 24 : block * 24 + 18]
        rest = ordered[144 + block * 24 : 144 + block * 24 + 18]
        share = ordered[288 + block * 24 : 288 + block * 24 + 18]
        for y in range(4):
            lanes = slice(y * 128, y * 128 + 128)
            rows = pl.ds(block * 4 + y, 18, stride=24)
            dense_f[rows, :] = head[:, lanes] + rest[:, lanes]
            dense_m[rows, :] = share[:, lanes]
            dense_z[rows, :] = head[:, lanes] * share[:, lanes]
    reverse = reverse_matrix()
    frozen[...] = jnp.dot(dense_z[...].astype(BF16), reverse, preferred_element_type=F32)

    def spread_frozen(time):
        rows = slice(time * 24, time * 24 + 24)
        frozen_x[time] = spread_rows(frozen[rows, :][1:23]).astype(BF16)

    repeat(18, spread_frozen)

    copies["w1"].wait()
    copies["bias"].wait()

    def first_layer(time):
        total = bias_ref[0:1, :]
        for first in range(3):
            block = frozen_x[time + first].reshape(320, 128)
            total = total + jnp.dot(
                block, w1_ref[first * 128 : first * 128 + 128, :], preferred_element_type=F32
            )
        for third, part in enumerate(shifted(jnp.tanh(total).reshape(20, 16, 128))):
            act1[time, :, :, :, third * 128 : third * 128 + 128] = part.reshape(10, 2, 16, 128)

    repeat(16, first_layer)

    copies["w2"].wait()

    def second_layer(step):
        total = pair_dot(act1, step * 2, 2, 9, w2_ref)
        for member in range(2):
            values = jnp.tanh(total[:, member * 128 : member * 128 + 128] + bias_ref[1:2, :])
            for third, part in enumerate(shifted(values.reshape(18, 16, 128))):
                act2[pl.ds(step * 2, 2), :, member, :, third * 128 : third * 128 + 128] = part.reshape(2, 9, 16, 128)

    repeat(7, second_layer)

    copies["w3"].wait()

    def third_layer(time):
        total = time_dot(act2, time, 288, w3_ref).reshape(18, 16, 128)
        total = total[0:16] + pltpu.roll(total[1:17], 112, 2) + pltpu.roll(total[2:18], 96, 2)
        scale, shift = gather_rows(total, 2)
        pre0[time] = scale + bias_ref[2:3, :]
        pre1[time] = shift + bias_ref[3:4, :]

    repeat(12, third_layer)

    def transform(time):
        rows = slice((time + 3) * 24, (time + 3) * 24 + 24)
        field = dense_f[rows, :][4:20]
        share = dense_m[rows, :][4:20]
        growth = jnp.exp(jnp.tanh(pre0[time]))
        flow[time] = share * field + (1.0 - share) * (field * growth + pre1[time])

    repeat(12, transform)

    def force_step(time):
        rows = slice((time + 4) * 24, (time + 4) * 24 + 24)
        field = dense_f[rows, :][5:19]
        share = dense_m[rows, :][5:19]
        here = flow[time + 1]
        lane = lax.broadcasted_iota(jnp.int32, (16, 128), 1) % 8
        around = flow[time] + flow[time + 2] + pltpu.roll(here, 8, 1) + pltpu.roll(here, 120, 1)
        around = around + jnp.where(lane == 0, pltpu.roll(here, 121, 1), pltpu.roll(here, 1, 1))
        around = around + jnp.where(lane == 7, pltpu.roll(here, 7, 1), pltpu.roll(here, 127, 1))
        around = around[1:15] + here[0:14] + here[2:16]
        mid = here[1:15]
        force = -0.5 * around + 1.8 * mid + 0.2 * mid * mid * mid
        scale = jnp.tanh(pre0[time + 1][1:15])
        growth = jnp.exp(scale)
        active = 1.0 - share
        empty = jnp.zeros((2, 128), F32)
        scale_c[time] = jnp.concatenate(
            [active * (force * field * growth - 1.0) * (1.0 - scale * scale), empty], axis=0
        )
        shift_c[time] = jnp.concatenate([active * force, empty], axis=0)
        direct[time] = force * (share + active * growth)

    repeat(10, force_step)
    scale_c[...] = jnp.dot(
        scale_c[...].reshape(160, 128).astype(BF16), reverse, preferred_element_type=F32
    ).reshape(10, 16, 128)
    shift_c[...] = jnp.dot(
        shift_c[...].reshape(160, 128).astype(BF16), reverse, preferred_element_type=F32
    ).reshape(10, 16, 128)

    def spread_third(time):
        third_x[time, :, :, 0:128] = spread_rows(scale_c[time][0:14]).astype(BF16)
        third_x[time, :, :, 128:256] = spread_rows(shift_c[time][0:14]).astype(BF16)

    repeat(10, spread_third)

    copies["w3t"].wait()

    def second_cot(time):
        total = None
        for first in range(3):
            block = third_x[time + first].reshape(192, 256)
            term = jnp.dot(
                block, w3t_ref[first * 256 : first * 256 + 256, :], preferred_element_type=F32
            )
            total = term if total is None else total + term
        act = act2[time + 3, :, :, :, 128:256].reshape(18, 16, 128)[3:15].astype(F32)
        values = total.reshape(12, 16, 128) * (1.0 - act * act)
        for third, part in enumerate(shifted(values)):
            cot2[time, :, :, :, third * 128 : third * 128 + 128] = part.reshape(6, 2, 16, 128)

    repeat(8, second_cot)

    copies["w2t"].wait()

    def first_cot(step):
        total = pair_dot(cot2, step * 2, 2, 5, w2t_ref)
        for member in range(2):
            act = act1[pl.ds(step * 2 + 5, 2), 2 + member : 7 + member, 1 - member, :, 128:256]
            act = act.astype(F32).reshape(10, 16, 128)
            values = total[:, member * 128 : member * 128 + 128].reshape(10, 16, 128) * (1.0 - act * act)
            for third, part in enumerate(shifted(values)):
                cot1[pl.ds(step * 2, 2), :, member, :, third * 128 : third * 128 + 128] = part.reshape(2, 5, 16, 128)

    repeat(3, first_cot)

    sent = pltpu.make_async_copy(cot1, cot1_hbm, sems.at[7])
    sent.start()
    for time in range(4):
        rows = slice(time * 8, time * 8 + 8)
        held[0, rows, :] = flow[time + 4][4:12]
        held[1, rows, :] = direct[time + 3][3:11]
        held[2, rows, :] = dense_m[(time + 7) * 24 + 8 : (time + 7) * 24 + 16, :]

    def put(block, values):
        out_ref[2 * block, :, :] = values[0:8]
        out_ref[2 * block + 1, :, :] = values[8:16]

    own2 = cot2[2:6, 1:5, :, :, 128:256].reshape(512, 128).astype(F32)
    own1 = cot1[1:5, :, :, :, 128:256].reshape(4, 10, 16, 128)[:, 1:9].reshape(512, 128).astype(F32)
    own_a = act2[5:9, :, :, :, 128:256].reshape(4, 18, 16, 128)[:, 5:13].reshape(512, 128).astype(F32)
    turn2 = own2.T.astype(BF16)
    turn1 = own1.T.astype(BF16)
    turn_a = own_a.T.astype(BF16)
    zone = lax.broadcasted_iota(jnp.int32, (16, 128), 1)

    def lane_sum(values, lanes_zone, shift):
        total = jnp.zeros((16, 128), F32)
        for z in range(8):
            total = total + jnp.where(lanes_zone == (z + shift) % 8, values[z * 16 : z * 16 + 16], 0.0)
        return total

    packed = [None] * 11
    for first in range(3):
        for second in range(3):
            low = (5 + second) // 2
            block = act1[5 + first : 9 + first, low : low + 5].reshape(4, 10, 16, 384)
            start = 5 + second - 2 * low
            block = block[:, start : start + 8].reshape(512, 384)
            product = jnp.dot(turn2, block, preferred_element_type=F32)
            for third in range(3):
                for ez in range(3):
                    number = ((third * 3 + second) * 3 + ez) * 3 + first
                    part = lane_sum(product[:, third * 128 : third * 128 + 128], zone // 16, ez - 1)
                    for step in (64, 32, 16):
                        part = part + pltpu.roll(part, step, 1)
                    old = packed[number // 8]
                    packed[number // 8] = (
                        part if old is None else jnp.where(zone // 16 == number % 8, part, old)
                    )
    for number in range(11):
        put(number, packed[number])

    extra = jnp.zeros((16, 128), F32)
    for first in range(3):
        block = third_x[2 + first : 6 + first, 2:10].reshape(512, 256)
        product = jnp.dot(turn_a, block, preferred_element_type=F32)
        total = jnp.zeros((16, 128), F32)
        for o in range(2):
            for ez in range(3):
                part = fold_group(lane_sum(product[:, o * 128 : o * 128 + 128], zone % 8, 1 - ez))
                total = jnp.where(zone % 8 == o * 3 + ez, part, total)
        block = frozen_x[6 + first : 10 + first, 6:14].reshape(512, 128)
        product = jnp.dot(turn1, block, preferred_element_type=F32)
        for ez in range(3):
            part = fold_group(lane_sum(product, zone % 8, ez - 1))
            if ez < 2:
                total = jnp.where(zone % 8 == 6 + ez, part, total)
            else:
                extra = jnp.where(zone % 8 == first, part, extra)
        put(11 + first, total)
    put(14, extra)
    sums = [
        jnp.sum(own1, axis=0, keepdims=True),
        jnp.sum(own2, axis=0, keepdims=True),
        jnp.sum(jnp.sum(scale_c[3:7], axis=0)[3:11], axis=0, keepdims=True),
        jnp.sum(jnp.sum(shift_c[3:7], axis=0)[3:11], axis=0, keepdims=True),
    ]
    site = lax.broadcasted_iota(jnp.int32, (16, 128), 0)
    total = jnp.zeros((16, 128), F32)
    for row, value in enumerate(sums):
        total = jnp.where(site == row, jnp.broadcast_to(value, (16, 128)), total)
    put(15, total)
    sent.wait()


def input_grad_kernel(
    cot1_hbm, held_ref, w1t_hbm, perm_hbm, out_ref, own_out, rows_out, cot1_ref, w1t_ref, perm_ref, sems
):
    copies = [
        pltpu.make_async_copy(cot1_hbm, cot1_ref, sems.at[0]),
        pltpu.make_async_copy(w1t_hbm, w1t_ref, sems.at[1]),
        pltpu.make_async_copy(perm_hbm, perm_ref, sems.at[2]),
    ]
    for copy in copies:
        copy.start()
    for copy in copies:
        copy.wait()
    for time in range(4):
        total = time_dot(cot1_ref, time, 160, w1t_ref).reshape(10, 16, 128)
        total = total[0:8] + pltpu.roll(total[1:9], 120, 2) + pltpu.roll(total[2:10], 112, 2)
        (total,) = gather_rows(total, 1)
        rows = slice(time * 8, time * 8 + 8)
        own_out[rows, :] = held_ref[0, rows, :]
        own_out[32 + time * 8 : 40 + time * 8, :] = held_ref[1, rows, :] + held_ref[2, rows, :] * total
    for kind in range(2):
        for half in range(2):
            for y in range(4):
                rows_out[(kind * 2 + half) * 4 : (kind * 2 + half) * 4 + 4, y * 128 : y * 128 + 128] = own_out[
                    pl.ds(kind * 32 + half * 4 + y, 4, stride=8), :
                ]
    ordered = split_dot(rows_out[...], perm_ref[...], 3, transposed=True)
    for target in range(32):
        spot, half = target // 2, target % 2
        lanes = slice(spot * 32, spot * 32 + 32)
        out_ref[target] = jnp.zeros((8, 128), F32)
        out_ref[target, 0:4, 0:32] = ordered[half * 4 : half * 4 + 4, lanes]
        out_ref[target, 0:4, 32:64] = ordered[8 + half * 4 : 12 + half * 4, lanes]


def unpack_kernel(in_ref, flowed_ref, grad_ref, g1_ref, g2_ref, g3_ref, b1_ref, b2_ref, b3_ref, window, extra, turned_x):
    for source in range(32):
        window[4 * source : 4 * source + 4, :] = in_ref[source, 8:12, :]
    turned = window[...].T
    flowed_ref[...] = turned[0:32]
    grad_ref[...] = turned[32:64]

    def group(number):
        return jnp.concatenate([in_ref[2 * number, 0:8, :], in_ref[2 * number + 1, 0:8, :]], axis=0)

    for number in range(11):
        block = group(number)
        for slot in range(min(8, 81 - number * 8)):
            g2_ref[number * 8 + slot] = block[:, slot * 16 : slot * 16 + 16]
    for number in range(4):
        extra[number * 16 : number * 16 + 16, :] = group(11 + number)
    extra[64:128, :] = jnp.zeros((64, 128), F32)
    turned_x[...] = extra[...].T
    for et in range(3):
        lanes = slice(et * 16, et * 16 + 16)
        for ey in range(3):
            for ex in range(3):
                for ez in range(3):
                    off = ((ex * 3 + ey) * 3 + ez) * 3
                    row = ey * 24 + (2 - ex) * 8
                    if ez < 2:
                        g1_ref[off + et] = turned_x[row + 6 + ez : row + 7 + ez, lanes]
                    else:
                        g1_ref[off + et] = turned_x[row + et : row + et + 1, 48:64]
                    row = (2 - ey) * 24 + ex * 8 + ez
                    g3_ref[off + 2 - et, 0:1, :] = turned_x[row : row + 1, lanes]
                    g3_ref[off + 2 - et, 1:2, :] = turned_x[row + 3 : row + 4, lanes]
    sums = in_ref[30, 0:8, :]
    lane = lax.broadcasted_iota(jnp.int32, (1, 128), 1)
    total = jnp.sum(sums, axis=1, keepdims=True)
    b3_ref[...] = jnp.where(lane == 0, total[2:3], total[3:4])[:, 0:2]
    for step in (64, 32, 16):
        sums = sums + pltpu.roll(sums, step, 1)
    b1_ref[...] = sums[0:1, 0:16]
    b2_ref[...] = sums[1:2, 0:16]


def ring(count, step):
    return [(i, (i + step) % count) for i in range(count)]


def shape(dims, dtype=F32):
    return jax.ShapeDtypeStruct(dims, dtype)


def run_weights(kernel_one, bias_one, kernel_two, bias_two, kernel_three, bias_three):
    return pl.pallas_call(
        weights_kernel,
        out_shape=[
            shape((384, 128), BF16),
            shape((768, 128), BF16),
            shape((4608, 256), BF16),
            shape((4608, 256), BF16),
            shape((1152, 128), BF16),
            shape((1152, 128), BF16),
            shape((4, 128)),
        ],
        in_specs=[VMEM_SPEC] * 6,
        out_specs=[HBM_SPEC] * 7,
        scratch_shapes=[
            pltpu.VMEM((384, 128), BF16),
            pltpu.VMEM((768, 128), BF16),
            pltpu.VMEM((4608, 256), BF16),
            pltpu.VMEM((4608, 256), BF16),
            pltpu.VMEM((1152, 128), BF16),
            pltpu.VMEM((1152, 128), BF16),
            pltpu.VMEM((4, 128), F32),
            pltpu.VMEM((81, 128), F32),
            pltpu.VMEM((1296, 128), F32),
            pltpu.VMEM((162, 128), F32),
            pltpu.SemaphoreType.DMA((7,)),
        ],
        compiler_params=pltpu.CompilerParams(vmem_limit_bytes=60 * 2**20),
        cost_estimate=pl.CostEstimate(flops=10**6, bytes_accessed=8 * 10**6, transcendentals=0),
        name="weights",
    )(
        kernel_one[:, 0].transpose(1, 2, 3, 4, 0).reshape(81, 16),
        kernel_two.transpose(2, 3, 4, 5, 0, 1).reshape(1296, 16),
        kernel_three.transpose(2, 3, 4, 5, 0, 1).reshape(162, 16),
        bias_one.reshape(1, 16),
        bias_two.reshape(1, 16),
        bias_three.reshape(1, 2),
    )


def run_main(*operands, name="flow"):
    return pl.pallas_call(
        main_kernel,
        out_shape=[
            shape((32, 8, 128)),
            shape((6, 5, 2, 16, 384), BF16),
            shape((3, 32, 128)),
        ],
        in_specs=[VMEM_SPEC] + [HBM_SPEC] * 7,
        out_specs=[VMEM_SPEC, HBM_SPEC, VMEM_SPEC],
        scratch_shapes=[
            pltpu.VMEM((18, 24, 512), F32),
            pltpu.VMEM((432, 128), F32),
            pltpu.VMEM((432, 128), F32),
            pltpu.VMEM((432, 128), F32),
            pltpu.VMEM((432, 128), F32),
            pltpu.VMEM((18, 20, 16, 128), BF16),
            pltpu.VMEM((16, 10, 2, 16, 384), BF16),
            pltpu.VMEM((14, 9, 2, 16, 384), BF16),
            pltpu.VMEM((12, 16, 128), F32),
            pltpu.VMEM((12, 16, 128), F32),
            pltpu.VMEM((12, 16, 128), F32),
            pltpu.VMEM((10, 16, 128), F32),
            pltpu.VMEM((10, 16, 128), F32),
            pltpu.VMEM((10, 14, 128), F32),
            pltpu.VMEM((10, 12, 16, 256), BF16),
            pltpu.VMEM((8, 6, 2, 16, 384), BF16),
            pltpu.VMEM((6, 5, 2, 16, 384), BF16),
            pltpu.VMEM((512, 512), BF16),
            pltpu.VMEM((384, 128), BF16),
            pltpu.VMEM((768, 128), BF16),
            pltpu.VMEM((4608, 256), BF16),
            pltpu.VMEM((4608, 256), BF16),
            pltpu.VMEM((1152, 128), BF16),
            pltpu.VMEM((4, 128), F32),
            pltpu.SemaphoreType.DMA((8,)),
        ],
        compiler_params=pltpu.CompilerParams(vmem_limit_bytes=60 * 2**20),
        cost_estimate=pl.CostEstimate(flops=2 * 10**10, bytes_accessed=8 * 10**6, transcendentals=10**6),
        name=name,
    )(*operands)


def main_shapes():
    return [
        shape((32, 48, 128), BF16), shape((512, 512), BF16), shape((384, 128), BF16), shape((768, 128), BF16),
        shape((4608, 256), BF16), shape((4608, 256), BF16), shape((1152, 128), BF16), shape((4, 128)),
    ]


def local(field, parity_mask, kernel_one, bias_one, kernel_two, bias_two, kernel_three, bias_three):
    own = pl.pallas_call(
        split_kernel,
        out_shape=shape((96, 128), BF16),
        in_specs=[VMEM_SPEC] * 2,
        out_specs=VMEM_SPEC,
        name="split",
    )(field.reshape(32, 128), parity_mask.reshape(32, 128))
    low = lax.ppermute(own, "gyh", ring(8, 1))
    high = lax.ppermute(own, "gyh", ring(8, -1))
    packed = pl.pallas_call(
        pack_kernel,
        out_shape=shape((32, 48, 128), BF16),
        in_specs=[VMEM_SPEC] * 3,
        out_specs=VMEM_SPEC,
        scratch_shapes=[pltpu.VMEM((6, 144, 128), F32)],
        name="pack",
    )(low, own, high)
    gathered = lax.all_to_all(packed, GROUP, 0, 0)
    w1, w3t, w2, w2t, w3, w1t, bias = run_weights(
        kernel_one, bias_one, kernel_two, bias_two, kernel_three, bias_three
    )
    perm = jnp.asarray(lane_permutation(), BF16)
    shares, cot1, held = run_main(gathered, perm, w1, w3t, w2, w2t, w3, bias)
    shares = lax.all_to_all(shares, GROUP, 0, 0)
    outputs = pl.pallas_call(
        input_grad_kernel,
        out_shape=shape((32, 8, 128)),
        in_specs=[HBM_SPEC, VMEM_SPEC, HBM_SPEC, HBM_SPEC],
        out_specs=VMEM_SPEC,
        scratch_shapes=[
            pltpu.VMEM((64, 128), F32),
            pltpu.VMEM((16, 512), F32),
            pltpu.VMEM((6, 5, 2, 16, 384), BF16),
            pltpu.VMEM((1152, 128), BF16),
            pltpu.VMEM((512, 512), BF16),
            pltpu.SemaphoreType.DMA((3,)),
        ],
        compiler_params=pltpu.CompilerParams(vmem_limit_bytes=60 * 2**20),
        cost_estimate=pl.CostEstimate(flops=5 * 10**8, bytes_accessed=3 * 10**6, transcendentals=0),
        name="input_grad",
    )(cot1, held, w1t, perm)
    share = jnp.broadcast_to(jnp.sum(shares, axis=0)[None], (8, 8, 128))
    share = lax.all_to_all(share, "gyh", 0, 0)
    share = jnp.sum(share, axis=0) * (1.0 / VOLUME)
    last = jnp.concatenate([jnp.broadcast_to(share[None], (32, 8, 128)), outputs], axis=1)
    last = lax.all_to_all(last, GROUP, 0, 0)
    flowed, field_grad, g1, g2, g3, b1, b2, b3 = pl.pallas_call(
        unpack_kernel,
        out_shape=[
            shape((32, 128)), shape((32, 128)), shape((81, 1, 16)), shape((81, 16, 16)), shape((81, 2, 16)),
            shape((1, 16)), shape((1, 16)), shape((1, 2)),
        ],
        in_specs=[VMEM_SPEC],
        out_specs=[VMEM_SPEC] * 8,
        scratch_shapes=[pltpu.VMEM((128, 128), F32), pltpu.VMEM((128, 128), F32), pltpu.VMEM((128, 128), F32)],
        name="unpack",
    )(last)
    return (
        flowed.reshape(2, 4, 4, 128),
        field_grad.reshape(2, 4, 4, 128),
        g1.reshape(3, 3, 3, 3, 1, 16).transpose(5, 4, 0, 1, 2, 3),
        b1.reshape(16),
        g2.reshape(3, 3, 3, 3, 16, 16).transpose(4, 5, 0, 1, 2, 3),
        b2.reshape(16),
        g3.reshape(3, 3, 3, 3, 2, 16).transpose(4, 5, 0, 1, 2, 3),
        b3.reshape(2),
    )


def solution(mesh):
    split = Mesh(mesh.devices.reshape(8, 8, 2, 2), ("gx", "gyh", "gyl", "gz"))
    block = P("gx", ("gyh", "gyl"), "gz", None)
    return jax.shard_map(
        local,
        mesh=split,
        in_specs=(block, block, P(), P(), P(), P(), P(), P()),
        out_specs=(block, block, P(), P(), P(), P(), P(), P()),
        check_vma=False,
    )
```

```python
import functools

import jax
import jax.numpy as jnp
import numpy as np
from jax import lax
from jax.experimental import pallas as pl
from jax.experimental.pallas import tpu as pltpu
from jax.sharding import Mesh
from jax.sharding import PartitionSpec as P

F32 = jnp.float32
BF16 = jnp.bfloat16
GROUP = ("gz", "gx", "gyl")
VMEM_SPEC = pl.BlockSpec(memory_space=pltpu.VMEM)
HBM_SPEC = pl.BlockSpec(memory_space=pltpu.HBM)
VOLUME = 1048576.0


def lane_permutation():
    matrix = np.zeros((512, 512), np.float32)
    for gz in range(2):
        for gx in range(8):
            for x in range(2):
                for y in range(4):
                    for z in range(4):
                        source = (gz * 8 + gx) * 32 + x * 16 + y * 4 + z
                        target = y * 128 + (gx * 2 + x) * 8 + gz * 4 + z
                        matrix[source, target] = 1.0
    return matrix


def pack_kernel(field_ref, mask_ref, out_ref, window):
    field = field_ref[...]
    head = field.astype(BF16).astype(F32)
    empty = jnp.zeros((32, 128), F32)
    both = jnp.concatenate([head, field - head, mask_ref[...].astype(F32)], axis=0)
    near = jnp.concatenate([pltpu.roll(both, 7, 1), empty], axis=0).T
    later = jnp.concatenate([empty, pltpu.roll(both, 119, 1)], axis=0).T
    lane = lax.broadcasted_iota(jnp.int32, (128, 128), 1)
    rows = [near]
    for kind in range(3):
        turned = pltpu.roll(later, 64 - 32 * kind, 1)
        rows.append(jnp.where(lane < 96, near, pltpu.roll(turned, 2 * kind, 0)))
    for number in range(1, 4):
        window[number - 1, 0:128, :] = rows[number]
        window[number - 1, 128:144, :] = rows[number][0:16, :]
    row = lax.broadcasted_iota(jnp.int32, (16, 128), 0)
    for slot in range(32):
        here = slice(4 * slot, 4 * slot + 16)
        out_ref[slot] = jnp.where(
            row < 2, window[0, here, :], jnp.where(row < 4, window[1, here, :], window[2, here, :])
        ).astype(BF16)


def tile_dot(values):
    spot = lax.broadcasted_iota(jnp.int32, (16, 128), 0)
    lane = lax.broadcasted_iota(jnp.int32, (16, 128), 1)
    return jnp.dot(values, jnp.where(lane % 16 == spot, 1.0, 0.0).astype(BF16), preferred_element_type=F32)


def weights_kernel(
    k1_ref, k2_ref, k3_ref, b1_ref, b2_ref, b3_ref,
    w1_hbm, w3t_hbm, w2_hbm, w2t_hbm, w3_hbm, w1t_hbm, bias_hbm,
    w1_ref, w3t_ref, w2_ref, w2t_ref, w3_ref, w1t_ref, bias_ref, one, two, three, sems,
):
    def at(ex, ey, ez, et):
        return ((ex * 3 + ey) * 3 + ez) * 3 + et

    one[...] = tile_dot(k1_ref[...])
    two[...] = tile_dot(k2_ref[...])
    three[...] = tile_dot(k3_ref[...])
    zone = lax.broadcasted_iota(jnp.int32, (8, 128), 1) // 16
    spot = lax.broadcasted_iota(jnp.int32, (8, 128), 0)
    wide = lax.broadcasted_iota(jnp.int32, (16, 128), 1) // 16
    zeros = jnp.zeros((128, 128), BF16)

    def rows8(ref, base, ex, ey, et, ahead):
        total = jnp.zeros((8, 128), F32)
        for ez in range(3):
            value = jnp.broadcast_to(ref[base(at(ex, ey, ez, et)), :], (8, 128))
            total = jnp.where(zone == (spot + ahead * (ez - 1) + 8) % 8, value, total)
        return total

    def row_one(off):
        return slice(off, off + 1)

    def row_three(o):
        return lambda off: slice(off * 2 + o, off * 2 + o + 1)

    for et in range(3):
        w1_ref[et * 128 + 72 : et * 128 + 128, :] = jnp.zeros((56, 128), BF16)
        for ey in range(3):
            block = [rows8(one, row_one, 2 - turned, ey, et, -1) for turned in range(3)]
            w1_ref[et * 128 + ey * 24 : et * 128 + ey * 24 + 24, :] = jnp.concatenate(block, axis=0).astype(BF16)
        for o in range(2):
            base = (et * 2 + o) * 128
            w3t_ref[base + 72 : base + 128, :] = jnp.zeros((56, 128), BF16)
            for dy in range(3):
                block = [rows8(three, row_three(o), turned, 2 - dy, 2 - et, 1) for turned in range(3)]
                w3t_ref[base + dy * 24 : base + dy * 24 + 24, :] = jnp.concatenate(block, axis=0).astype(BF16)
        for ex in range(3):
            block = []
            for ey in range(3):
                for o in range(2):
                    block.append(rows8(three, row_three(o), ex, ey, et, 1))
            block.append(jnp.zeros((80, 128), F32))
            rows = slice((et * 3 + ex) * 128, (et * 3 + ex) * 128 + 128)
            w3_ref[rows, :] = jnp.concatenate(block, axis=0).T.astype(BF16)
            block = [rows8(one, row_one, 2 - ex, 2 - dy, 2 - et, -1) for dy in range(3)]
            block.append(jnp.zeros((104, 128), F32))
            w1t_ref[rows, :] = jnp.concatenate(block, axis=0).T.astype(BF16)
            for ey in range(3):
                parts = [two[at(ex, ey, ez, et) * 16 : at(ex, ey, ez, et) * 16 + 16, :] for ez in range(3)]
                block = []
                for z in range(8):
                    total = jnp.zeros((16, 128), F32)
                    for ez in range(3):
                        total = jnp.where(wide == (z + ez - 1) % 8, parts[ez], total)
                    block.append(total)
                block = jnp.concatenate(block, axis=0)
                turned = block.T.astype(BF16)
                block = block.astype(BF16)
                for member in range(2):
                    lanes = slice(member * 128, member * 128 + 128)
                    base = ((et * 4 + ey + member) * 3 + ex) * 128
                    w2_ref[base : base + 128, lanes] = turned
                    base = (((2 - et) * 4 + 2 - ey + member) * 3 + 2 - ex) * 128
                    w2t_ref[base : base + 128, lanes] = block
            for member in range(2):
                lanes = slice(member * 128, member * 128 + 128)
                base = ((et * 4 + 3 * (1 - member)) * 3 + ex) * 128
                w2_ref[base : base + 128, lanes] = zeros
                w2t_ref[base : base + 128, lanes] = zeros
    bias_ref[0:1, :] = jnp.concatenate([b1_ref[...]] * 8, axis=1)
    bias_ref[1:2, :] = jnp.concatenate([b2_ref[...]] * 8, axis=1)
    bias_ref[2:3, :] = jnp.broadcast_to(b3_ref[0:1, 0:1], (1, 128))
    bias_ref[3:4, :] = jnp.broadcast_to(b3_ref[0:1, 1:2], (1, 128))
    copies = []
    for number, (source, target) in enumerate(
        (
            (w1_ref, w1_hbm),
            (w3t_ref, w3t_hbm),
            (w2_ref, w2_hbm),
            (w2t_ref, w2t_hbm),
            (w3_ref, w3_hbm),
            (w1t_ref, w1t_hbm),
            (bias_ref, bias_hbm),
        )
    ):
        copies.append(pltpu.make_async_copy(source, target, sems.at[number]))
        copies[-1].start()
    for copy in copies:
        copy.wait()


def split_dot(values, matrix, parts, transposed=False):
    dims = (((1,), (1 if transposed else 0,)), ((), ()))
    total = None
    rest = values
    for _ in range(parts):
        head = rest.astype(BF16)
        rest = rest - head.astype(F32)
        term = lax.dot_general(head, matrix, dims, preferred_element_type=F32)
        total = term if total is None else total + term
    return total


def reverse_matrix():
    source = lax.broadcasted_iota(jnp.int32, (128, 128), 0)
    target = lax.broadcasted_iota(jnp.int32, (128, 128), 1)
    return jnp.where(source == (15 - target // 8) * 8 + target % 8, 1.0, 0.0).astype(BF16)


def spread_rows(values):
    count = values.shape[0] - 2
    site = lax.broadcasted_iota(jnp.int32, (count, 16, 128), 1)
    lane = (lax.broadcasted_iota(jnp.int32, (count, 16, 128), 2) + 8 * site) % 128
    pieces = []
    for second in range(3):
        turned = pltpu.roll(values, 16 + 24 * second, 1)[second : second + count]
        pieces.append(jnp.broadcast_to(turned[:, None, :], (count, 16, 128)))
    wide = jnp.where(lane < 24, pieces[0], jnp.where(lane < 48, pieces[1], pieces[2]))
    return pltpu.roll(wide, 0, 2, stride=8, stride_axis=1)


def gather_rows(values, place):
    count = values.shape[0]
    site = lax.broadcasted_iota(jnp.int32, (count, 16, 128), 1)
    lane = lax.broadcasted_iota(jnp.int32, (count, 16, 128), 2) // 8
    moved = pltpu.roll(values, 0, 2, stride=8, stride_axis=1)
    results = []
    for spot in range(place):
        total = jnp.sum(jnp.where(lane == (site + spot) % 16, moved, 0.0), axis=1)
        results.append(total if spot == 0 else pltpu.roll(total, 128 - 8 * spot, 1))
    return results


def shifted(values):
    return (
        pltpu.roll(values, 1, 1).astype(BF16),
        values.astype(BF16),
        pltpu.roll(values, 15, 1).astype(BF16),
    )


def pair_dot(ref, time, steps, pairs, w_ref):
    total = None
    for first in range(3):
        for start in range(2):
            sides = []
            for block in (2 * start, 2 * start + 1):
                rows = ref[pl.ds(time + first, steps), block // 2 : block // 2 + pairs, block % 2]
                sides.append(rows.reshape(steps * pairs * 16, 384))
            at = (first * 2 + start) * 768
            term = jnp.dot(
                jnp.concatenate(sides, axis=1), w_ref[at : at + 768, :], preferred_element_type=F32
            )
            total = term if total is None else total + term
    return total


def time_dot(ref, time, rows, w_ref):
    sides = [ref[time + first].reshape(rows, ref.shape[-1]) for first in range(3)]
    return jnp.dot(jnp.concatenate(sides, axis=1), w_ref[...], preferred_element_type=F32)


def fold_group(values):
    lane = lax.broadcasted_iota(jnp.int32, values.shape, 1)
    for step in (1, 2, 4):
        down = pltpu.roll(values, 128 - step, 1)
        up = pltpu.roll(values, step, 1)
        values = values + jnp.where((lane // step) % 2 == 0, down, up)
    return values


def main_kernel(
    low_ref, own_ref, high_ref, perm_hbm, w1_hbm, w3t_hbm, w2_hbm, w2t_hbm, w3_hbm, bias_hbm,
    out_ref, cot1_hbm, held,
    gather, dense_f, dense_m, dense_z, frozen, frozen_x, act1, act2, pre0, pre1, flow, scale_c, shift_c,
    direct, third_x, cot2, cot1, perm_ref, w1_ref, w3t_ref, w2_ref, w2t_ref, w3_ref, bias_ref, sems,
):
    copies = {}
    for number, (name, source, target) in enumerate(
        (
            ("perm", perm_hbm, perm_ref),
            ("w1", w1_hbm, w1_ref),
            ("bias", bias_hbm, bias_ref),
            ("w2", w2_hbm, w2_ref),
            ("w3", w3_hbm, w3_ref),
            ("w3t", w3t_hbm, w3t_ref),
            ("w2t", w2t_hbm, w2t_ref),
        )
    ):
        copies[name] = pltpu.make_async_copy(source, target, sems.at[number])
        copies[name].start()

    def repeat(count, body):
        for step in range(count):
            body(step)

    for block, ref in enumerate((own_ref, low_ref, high_ref)):
        block = (1, 0, 2)[block]
        for source in range(32):
            spot, half = source // 2, source % 2
            lanes = slice(spot * 32, spot * 32 + 32)
            tile = ref[source].astype(F32)
            for kind in range(3):
                place = kind * 6 + block * 2 + half
                gather[place, 0:16, lanes] = tile[:, 32 * kind : 32 * kind + 32]
                gather[place, 16:18, lanes] = tile[2 * kind : 2 * kind + 2, 96:128]
    copies["perm"].wait()
    ordered = jnp.dot(
        gather[...].reshape(432, 512).astype(BF16), perm_ref[...], preferred_element_type=F32
    )
    for block in range(6):
        head = ordered[block * 24 : block * 24 + 18]
        rest = ordered[144 + block * 24 : 144 + block * 24 + 18]
        share = ordered[288 + block * 24 : 288 + block * 24 + 18]
        for y in range(4):
            lanes = slice(y * 128, y * 128 + 128)
            rows = pl.ds(block * 4 + y, 18, stride=24)
            dense_f[rows, :] = head[:, lanes] + rest[:, lanes]
            dense_m[rows, :] = share[:, lanes]
            dense_z[rows, :] = head[:, lanes] * share[:, lanes]
    reverse = reverse_matrix()
    frozen[...] = jnp.dot(dense_z[...].astype(BF16), reverse, preferred_element_type=F32)

    def spread_frozen(time):
        rows = slice(time * 24, time * 24 + 24)
        frozen_x[time] = spread_rows(frozen[rows, :][1:23]).astype(BF16)

    repeat(18, spread_frozen)

    copies["w1"].wait()
    copies["bias"].wait()

    def first_layer(time):
        total = time_dot(frozen_x, time, 320, w1_ref) + bias_ref[0:1, :]
        for third, part in enumerate(shifted(jnp.tanh(total).reshape(20, 16, 128))):
            act1[time, :, :, :, third * 128 : third * 128 + 128] = part.reshape(10, 2, 16, 128)

    repeat(16, first_layer)

    copies["w2"].wait()

    def second_layer(step):
        total = pair_dot(act1, step * 1, 1, 9, w2_ref)
        for member in range(2):
            values = jnp.tanh(total[:, member * 128 : member * 128 + 128] + bias_ref[1:2, :])
            for third, part in enumerate(shifted(values.reshape(9, 16, 128))):
                act2[pl.ds(step * 1, 1), :, member, :, third * 128 : third * 128 + 128] = part.reshape(1, 9, 16, 128)

    repeat(14, second_layer)

    copies["w3"].wait()

    def third_layer(time):
        total = time_dot(act2, time, 288, w3_ref).reshape(18, 16, 128)
        total = total[0:16] + pltpu.roll(total[1:17], 112, 2) + pltpu.roll(total[2:18], 96, 2)
        scale, shift = gather_rows(total, 2)
        pre0[time] = scale + bias_ref[2:3, :]
        pre1[time] = shift + bias_ref[3:4, :]

    repeat(12, third_layer)

    def transform(time):
        rows = slice((time + 3) * 24, (time + 3) * 24 + 24)
        field = dense_f[rows, :][4:20]
        share = dense_m[rows, :][4:20]
        growth = jnp.exp(jnp.tanh(pre0[time]))
        flow[time] = share * field + (1.0 - share) * (field * growth + pre1[time])

    repeat(12, transform)

    def force_step(time):
        rows = slice((time + 4) * 24, (time + 4) * 24 + 24)
        field = dense_f[rows, :][5:19]
        share = dense_m[rows, :][5:19]
        here = flow[time + 1]
        lane = lax.broadcasted_iota(jnp.int32, (16, 128), 1) % 8
        around = flow[time] + flow[time + 2] + pltpu.roll(here, 8, 1) + pltpu.roll(here, 120, 1)
        around = around + jnp.where(lane == 0, pltpu.roll(here, 121, 1), pltpu.roll(here, 1, 1))
        around = around + jnp.where(lane == 7, pltpu.roll(here, 7, 1), pltpu.roll(here, 127, 1))
        around = around[1:15] + here[0:14] + here[2:16]
        mid = here[1:15]
        force = -0.5 * around + 1.8 * mid + 0.2 * mid * mid * mid
        scale = jnp.tanh(pre0[time + 1][1:15])
        growth = jnp.exp(scale)
        active = 1.0 - share
        empty = jnp.zeros((2, 128), F32)
        scale_c[time] = jnp.concatenate(
            [active * (force * field * growth - 1.0) * (1.0 - scale * scale), empty], axis=0
        )
        shift_c[time] = jnp.concatenate([active * force, empty], axis=0)
        direct[time] = force * (share + active * growth)

    repeat(10, force_step)
    scale_c[...] = jnp.dot(
        scale_c[...].reshape(160, 128).astype(BF16), reverse, preferred_element_type=F32
    ).reshape(10, 16, 128)
    shift_c[...] = jnp.dot(
        shift_c[...].reshape(160, 128).astype(BF16), reverse, preferred_element_type=F32
    ).reshape(10, 16, 128)

    def spread_third(time):
        third_x[time, :, :, 0:128] = spread_rows(scale_c[time][0:14]).astype(BF16)
        third_x[time, :, :, 128:256] = spread_rows(shift_c[time][0:14]).astype(BF16)

    repeat(10, spread_third)

    copies["w3t"].wait()

    def second_cot(time):
        total = time_dot(third_x, time, 192, w3t_ref)
        act = act2[time + 3, :, :, :, 128:256].reshape(18, 16, 128)[3:15].astype(F32)
        values = total.reshape(12, 16, 128) * (1.0 - act * act)
        for third, part in enumerate(shifted(values)):
            cot2[time, :, :, :, third * 128 : third * 128 + 128] = part.reshape(6, 2, 16, 128)

    repeat(8, second_cot)

    copies["w2t"].wait()

    def first_cot(step):
        total = pair_dot(cot2, step * 3, 3, 5, w2t_ref)
        for member in range(2):
            act = act1[pl.ds(step * 3 + 5, 3), 2 + member : 7 + member, 1 - member, :, 128:256]
            act = act.astype(F32).reshape(15, 16, 128)
            values = total[:, member * 128 : member * 128 + 128].reshape(15, 16, 128) * (1.0 - act * act)
            for third, part in enumerate(shifted(values)):
                cot1[pl.ds(step * 3, 3), :, member, :, third * 128 : third * 128 + 128] = part.reshape(3, 5, 16, 128)

    repeat(2, first_cot)

    sent = pltpu.make_async_copy(cot1, cot1_hbm, sems.at[7])
    sent.start()
    for time in range(4):
        rows = slice(time * 8, time * 8 + 8)
        held[0, rows, :] = flow[time + 4][4:12]
        held[1, rows, :] = direct[time + 3][3:11]
        held[2, rows, :] = dense_m[(time + 7) * 24 + 8 : (time + 7) * 24 + 16, :]

    def put(block, values):
        out_ref[2 * block, :, :] = values[0:8]
        out_ref[2 * block + 1, :, :] = values[8:16]

    own2 = cot2[2:6, 1:5, :, :, 128:256].reshape(512, 128).astype(F32)
    own1 = cot1[1:5, :, :, :, 128:256].reshape(4, 10, 16, 128)[:, 1:9].reshape(512, 128).astype(F32)
    own_a = act2[5:9, :, :, :, 128:256].reshape(4, 18, 16, 128)[:, 5:13].reshape(512, 128).astype(F32)
    turn2 = own2.T.astype(BF16)
    turn1 = own1.T.astype(BF16)
    turn_a = own_a.T.astype(BF16)
    zone = lax.broadcasted_iota(jnp.int32, (16, 128), 1)

    def lane_sum(values, lanes_zone, shift):
        total = jnp.zeros((16, 128), F32)
        for z in range(8):
            total = total + jnp.where(lanes_zone == (z + shift) % 8, values[z * 16 : z * 16 + 16], 0.0)
        return total

    packed = [None] * 11
    for first in range(3):
        for second in range(3):
            low = (5 + second) // 2
            block = act1[5 + first : 9 + first, low : low + 5].reshape(4, 10, 16, 384)
            start = 5 + second - 2 * low
            block = block[:, start : start + 8].reshape(512, 384)
            product = jnp.dot(turn2, block, preferred_element_type=F32)
            for third in range(3):
                for ez in range(3):
                    number = ((third * 3 + second) * 3 + ez) * 3 + first
                    part = lane_sum(product[:, third * 128 : third * 128 + 128], zone // 16, ez - 1)
                    for step in (64, 32, 16):
                        part = part + pltpu.roll(part, step, 1)
                    old = packed[number // 8]
                    packed[number // 8] = (
                        part if old is None else jnp.where(zone // 16 == number % 8, part, old)
                    )
    for number in range(11):
        put(number, packed[number])

    extra = jnp.zeros((16, 128), F32)
    for first in range(3):
        block = third_x[2 + first : 6 + first, 2:10].reshape(512, 256)
        product = jnp.dot(turn_a, block, preferred_element_type=F32)
        total = jnp.zeros((16, 128), F32)
        for o in range(2):
            for ez in range(3):
                part = fold_group(lane_sum(product[:, o * 128 : o * 128 + 128], zone % 8, 1 - ez))
                total = jnp.where(zone % 8 == o * 3 + ez, part, total)
        block = frozen_x[6 + first : 10 + first, 6:14].reshape(512, 128)
        product = jnp.dot(turn1, block, preferred_element_type=F32)
        for ez in range(3):
            part = fold_group(lane_sum(product, zone % 8, ez - 1))
            if ez < 2:
                total = jnp.where(zone % 8 == 6 + ez, part, total)
            else:
                extra = jnp.where(zone % 8 == first, part, extra)
        put(11 + first, total)
    put(14, extra)
    sums = [
        jnp.sum(own1, axis=0, keepdims=True),
        jnp.sum(own2, axis=0, keepdims=True),
        jnp.sum(jnp.sum(scale_c[3:7], axis=0)[3:11], axis=0, keepdims=True),
        jnp.sum(jnp.sum(shift_c[3:7], axis=0)[3:11], axis=0, keepdims=True),
    ]
    site = lax.broadcasted_iota(jnp.int32, (16, 128), 0)
    total = jnp.zeros((16, 128), F32)
    for row, value in enumerate(sums):
        total = jnp.where(site == row, jnp.broadcast_to(value, (16, 128)), total)
    put(15, total)
    sent.wait()


def input_grad_kernel(
    cot1_hbm, held_ref, w1t_hbm, perm_hbm, out_ref, own_out, rows_out, cot1_ref, w1t_ref, perm_ref, sems
):
    copies = [
        pltpu.make_async_copy(cot1_hbm, cot1_ref, sems.at[0]),
        pltpu.make_async_copy(w1t_hbm, w1t_ref, sems.at[1]),
        pltpu.make_async_copy(perm_hbm, perm_ref, sems.at[2]),
    ]
    for copy in copies:
        copy.start()
    for copy in copies:
        copy.wait()
    for time in range(4):
        total = time_dot(cot1_ref, time, 160, w1t_ref).reshape(10, 16, 128)
        total = total[0:8] + pltpu.roll(total[1:9], 120, 2) + pltpu.roll(total[2:10], 112, 2)
        (total,) = gather_rows(total, 1)
        rows = slice(time * 8, time * 8 + 8)
        own_out[rows, :] = held_ref[0, rows, :]
        own_out[32 + time * 8 : 40 + time * 8, :] = held_ref[1, rows, :] + held_ref[2, rows, :] * total
    for kind in range(2):
        for half in range(2):
            for y in range(4):
                rows_out[(kind * 2 + half) * 4 : (kind * 2 + half) * 4 + 4, y * 128 : y * 128 + 128] = own_out[
                    pl.ds(kind * 32 + half * 4 + y, 4, stride=8), :
                ]
    ordered = split_dot(rows_out[...], perm_ref[...], 3, transposed=True)
    for target in range(32):
        spot, half = target // 2, target % 2
        lanes = slice(spot * 32, spot * 32 + 32)
        out_ref[target] = jnp.zeros((8, 128), F32)
        out_ref[target, 0:4, 0:32] = ordered[half * 4 : half * 4 + 4, lanes]
        out_ref[target, 0:4, 32:64] = ordered[8 + half * 4 : 12 + half * 4, lanes]


def unpack_kernel(in_ref, flowed_ref, grad_ref, g1_ref, g2_ref, g3_ref, b1_ref, b2_ref, b3_ref, window, extra, turned_x):
    for source in range(32):
        window[4 * source : 4 * source + 4, :] = in_ref[source, 8:12, :]
    turned = window[...].T
    flowed_ref[...] = turned[0:32]
    grad_ref[...] = turned[32:64]

    def group(number):
        return jnp.concatenate([in_ref[2 * number, 0:8, :], in_ref[2 * number + 1, 0:8, :]], axis=0)

    for number in range(11):
        block = group(number)
        for slot in range(min(8, 81 - number * 8)):
            g2_ref[number * 8 + slot] = block[:, slot * 16 : slot * 16 + 16]
    for number in range(4):
        extra[number * 16 : number * 16 + 16, :] = group(11 + number)
    extra[64:128, :] = jnp.zeros((64, 128), F32)
    turned_x[...] = extra[...].T
    for et in range(3):
        lanes = slice(et * 16, et * 16 + 16)
        for ey in range(3):
            for ex in range(3):
                for ez in range(3):
                    off = ((ex * 3 + ey) * 3 + ez) * 3
                    row = ey * 24 + (2 - ex) * 8
                    if ez < 2:
                        g1_ref[off + et] = turned_x[row + 6 + ez : row + 7 + ez, lanes]
                    else:
                        g1_ref[off + et] = turned_x[row + et : row + et + 1, 48:64]
                    row = (2 - ey) * 24 + ex * 8 + ez
                    g3_ref[off + 2 - et, 0:1, :] = turned_x[row : row + 1, lanes]
                    g3_ref[off + 2 - et, 1:2, :] = turned_x[row + 3 : row + 4, lanes]
    sums = in_ref[30, 0:8, :]
    lane = lax.broadcasted_iota(jnp.int32, (1, 128), 1)
    total = jnp.sum(sums, axis=1, keepdims=True)
    b3_ref[...] = jnp.where(lane == 0, total[2:3], total[3:4])[:, 0:2]
    for step in (64, 32, 16):
        sums = sums + pltpu.roll(sums, step, 1)
    b1_ref[...] = sums[0:1, 0:16]
    b2_ref[...] = sums[1:2, 0:16]


def ring(count, step):
    return [(i, (i + step) % count) for i in range(count)]


def shape(dims, dtype=F32):
    return jax.ShapeDtypeStruct(dims, dtype)


def run_weights(kernel_one, bias_one, kernel_two, bias_two, kernel_three, bias_three):
    return pl.pallas_call(
        weights_kernel,
        out_shape=[
            shape((384, 128), BF16),
            shape((768, 128), BF16),
            shape((4608, 256), BF16),
            shape((4608, 256), BF16),
            shape((1152, 128), BF16),
            shape((1152, 128), BF16),
            shape((4, 128)),
        ],
        in_specs=[VMEM_SPEC] * 6,
        out_specs=[HBM_SPEC] * 7,
        scratch_shapes=[
            pltpu.VMEM((384, 128), BF16),
            pltpu.VMEM((768, 128), BF16),
            pltpu.VMEM((4608, 256), BF16),
            pltpu.VMEM((4608, 256), BF16),
            pltpu.VMEM((1152, 128), BF16),
            pltpu.VMEM((1152, 128), BF16),
            pltpu.VMEM((4, 128), F32),
            pltpu.VMEM((81, 128), F32),
            pltpu.VMEM((1296, 128), F32),
            pltpu.VMEM((162, 128), F32),
            pltpu.SemaphoreType.DMA((7,)),
        ],
        compiler_params=pltpu.CompilerParams(vmem_limit_bytes=60 * 2**20),
        cost_estimate=pl.CostEstimate(flops=10**6, bytes_accessed=8 * 10**6, transcendentals=0),
        name="weights",
    )(
        kernel_one[:, 0].transpose(1, 2, 3, 4, 0).reshape(81, 16),
        kernel_two.transpose(2, 3, 4, 5, 0, 1).reshape(1296, 16),
        kernel_three.transpose(2, 3, 4, 5, 0, 1).reshape(162, 16),
        bias_one.reshape(1, 16),
        bias_two.reshape(1, 16),
        bias_three.reshape(1, 2),
    )


def run_main(*operands, name="flow"):
    return pl.pallas_call(
        main_kernel,
        out_shape=[
            shape((32, 8, 128)),
            shape((6, 5, 2, 16, 384), BF16),
            shape((3, 32, 128)),
        ],
        in_specs=[VMEM_SPEC] * 3 + [HBM_SPEC] * 7,
        out_specs=[VMEM_SPEC, HBM_SPEC, VMEM_SPEC],
        scratch_shapes=[
            pltpu.VMEM((18, 24, 512), F32),
            pltpu.VMEM((432, 128), F32),
            pltpu.VMEM((432, 128), F32),
            pltpu.VMEM((432, 128), F32),
            pltpu.VMEM((432, 128), F32),
            pltpu.VMEM((18, 20, 16, 128), BF16),
            pltpu.VMEM((16, 10, 2, 16, 384), BF16),
            pltpu.VMEM((14, 9, 2, 16, 384), BF16),
            pltpu.VMEM((12, 16, 128), F32),
            pltpu.VMEM((12, 16, 128), F32),
            pltpu.VMEM((12, 16, 128), F32),
            pltpu.VMEM((10, 16, 128), F32),
            pltpu.VMEM((10, 16, 128), F32),
            pltpu.VMEM((10, 14, 128), F32),
            pltpu.VMEM((10, 12, 16, 256), BF16),
            pltpu.VMEM((8, 6, 2, 16, 384), BF16),
            pltpu.VMEM((6, 5, 2, 16, 384), BF16),
            pltpu.VMEM((512, 512), BF16),
            pltpu.VMEM((384, 128), BF16),
            pltpu.VMEM((768, 128), BF16),
            pltpu.VMEM((4608, 256), BF16),
            pltpu.VMEM((4608, 256), BF16),
            pltpu.VMEM((1152, 128), BF16),
            pltpu.VMEM((4, 128), F32),
            pltpu.SemaphoreType.DMA((8,)),
        ],
        compiler_params=pltpu.CompilerParams(vmem_limit_bytes=60 * 2**20),
        cost_estimate=pl.CostEstimate(flops=2 * 10**10, bytes_accessed=8 * 10**6, transcendentals=10**6),
        name=name,
    )(*operands)


def main_shapes():
    return [
        shape((32, 16, 128), BF16), shape((32, 16, 128), BF16), shape((32, 16, 128), BF16), shape((512, 512), BF16), shape((384, 128), BF16), shape((768, 128), BF16),
        shape((4608, 256), BF16), shape((4608, 256), BF16), shape((1152, 128), BF16), shape((4, 128)),
    ]


def local(field, parity_mask, kernel_one, bias_one, kernel_two, bias_two, kernel_three, bias_three):
    packed = pl.pallas_call(
        pack_kernel,
        out_shape=shape((32, 16, 128), BF16),
        in_specs=[VMEM_SPEC] * 2,
        out_specs=VMEM_SPEC,
        scratch_shapes=[pltpu.VMEM((3, 144, 128), F32)],
        name="pack",
    )(field.reshape(32, 128), parity_mask.reshape(32, 128))
    own = lax.all_to_all(packed, GROUP, 0, 0)
    low = lax.ppermute(own, "gyh", ring(8, 1))
    high = lax.ppermute(own, "gyh", ring(8, -1))
    w1, w3t, w2, w2t, w3, w1t, bias = run_weights(
        kernel_one, bias_one, kernel_two, bias_two, kernel_three, bias_three
    )
    perm = jnp.asarray(lane_permutation(), BF16)
    shares, cot1, held = run_main(low, own, high, perm, w1, w3t, w2, w2t, w3, bias)
    shares = lax.all_to_all(shares, GROUP, 0, 0)
    outputs = pl.pallas_call(
        input_grad_kernel,
        out_shape=shape((32, 8, 128)),
        in_specs=[HBM_SPEC, VMEM_SPEC, HBM_SPEC, HBM_SPEC],
        out_specs=VMEM_SPEC,
        scratch_shapes=[
            pltpu.VMEM((64, 128), F32),
            pltpu.VMEM((16, 512), F32),
            pltpu.VMEM((6, 5, 2, 16, 384), BF16),
            pltpu.VMEM((1152, 128), BF16),
            pltpu.VMEM((512, 512), BF16),
            pltpu.SemaphoreType.DMA((3,)),
        ],
        compiler_params=pltpu.CompilerParams(vmem_limit_bytes=60 * 2**20),
        cost_estimate=pl.CostEstimate(flops=5 * 10**8, bytes_accessed=3 * 10**6, transcendentals=0),
        name="input_grad",
    )(cot1, held, w1t, perm)
    share = jnp.broadcast_to(jnp.sum(shares, axis=0)[None], (8, 8, 128))
    share = lax.all_to_all(share, "gyh", 0, 0)
    share = jnp.sum(share, axis=0) * (1.0 / VOLUME)
    last = jnp.concatenate([jnp.broadcast_to(share[None], (32, 8, 128)), outputs], axis=1)
    last = lax.all_to_all(last, GROUP, 0, 0)
    flowed, field_grad, g1, g2, g3, b1, b2, b3 = pl.pallas_call(
        unpack_kernel,
        out_shape=[
            shape((32, 128)), shape((32, 128)), shape((81, 1, 16)), shape((81, 16, 16)), shape((81, 2, 16)),
            shape((1, 16)), shape((1, 16)), shape((1, 2)),
        ],
        in_specs=[VMEM_SPEC],
        out_specs=[VMEM_SPEC] * 8,
        scratch_shapes=[pltpu.VMEM((128, 128), F32), pltpu.VMEM((128, 128), F32), pltpu.VMEM((128, 128), F32)],
        name="unpack",
    )(last)
    return (
        flowed.reshape(2, 4, 4, 128),
        field_grad.reshape(2, 4, 4, 128),
        g1.reshape(3, 3, 3, 3, 1, 16).transpose(5, 4, 0, 1, 2, 3),
        b1.reshape(16),
        g2.reshape(3, 3, 3, 3, 16, 16).transpose(4, 5, 0, 1, 2, 3),
        b2.reshape(16),
        g3.reshape(3, 3, 3, 3, 2, 16).transpose(4, 5, 0, 1, 2, 3),
        b3.reshape(2),
    )


def solution(mesh):
    split = Mesh(mesh.devices.reshape(8, 8, 2, 2), ("gx", "gyh", "gyl", "gz"))
    block = P("gx", ("gyh", "gyl"), "gz", None)
    return jax.shard_map(
        local,
        mesh=split,
        in_specs=(block, block, P(), P(), P(), P(), P(), P()),
        out_specs=(block, block, P(), P(), P(), P(), P(), P()),
        check_vma=False,
    )
```

```python
import functools

import jax
import jax.numpy as jnp
from jax import lax
from jax.experimental import pallas as pl
from jax.experimental.pallas import tpu as pltpu
from jax.sharding import Mesh
from jax.sharding import PartitionSpec as P

F32 = jnp.float32
BF16 = jnp.bfloat16
GROUP = ("gz", "gx", "gyl")
VMEM_SPEC = pl.BlockSpec(memory_space=pltpu.VMEM)
VOLUME = 1048576.0


def pack_kernel(field_ref, mask_ref, out_ref, window):
    field = field_ref[...]
    head = field.astype(BF16).astype(F32)
    empty = jnp.zeros((32, 128), F32)
    both = jnp.concatenate([head, field - head, mask_ref[...].astype(F32)], axis=0)
    near = jnp.concatenate([pltpu.roll(both, 7, 1), empty], axis=0).T
    later = jnp.concatenate([empty, pltpu.roll(both, 119, 1)], axis=0).T
    lane = lax.broadcasted_iota(jnp.int32, (128, 128), 1)
    rows = [near]
    for kind in range(3):
        turned = pltpu.roll(later, 64 - 32 * kind, 1)
        rows.append(jnp.where(lane < 96, near, pltpu.roll(turned, 2 * kind, 0)))
    for number in range(1, 4):
        window[number - 1, 0:128, :] = rows[number]
        window[number - 1, 128:144, :] = rows[number][0:16, :]
    row = lax.broadcasted_iota(jnp.int32, (16, 128), 0)
    for slot in range(32):
        here = slice(4 * slot, 4 * slot + 16)
        out_ref[slot] = jnp.where(
            row < 2, window[0, here, :], jnp.where(row < 4, window[1, here, :], window[2, here, :])
        ).astype(BF16)


def tile_dot(values):
    spot = lax.broadcasted_iota(jnp.int32, (16, 128), 0)
    lane = lax.broadcasted_iota(jnp.int32, (16, 128), 1)
    return jnp.dot(values, jnp.where(lane % 16 == spot, 1.0, 0.0).astype(BF16), preferred_element_type=F32)


def weights_kernel(
    k1_ref, k2_ref, k3_ref, b1_ref, b2_ref, b3_ref,
    w1_ref, w3t_ref, w2_ref, w2t_ref, w3_ref, w1t_ref, bias_ref, perm_ref, one, two, three,
):
    def at(ex, ey, ez, et):
        return ((ex * 3 + ey) * 3 + ez) * 3 + et

    one[...] = tile_dot(k1_ref[...])
    two[...] = tile_dot(k2_ref[...])
    three[...] = tile_dot(k3_ref[...])
    zone = lax.broadcasted_iota(jnp.int32, (8, 128), 1) // 16
    spot = lax.broadcasted_iota(jnp.int32, (8, 128), 0)
    wide = lax.broadcasted_iota(jnp.int32, (16, 128), 1) // 16
    zeros = jnp.zeros((128, 128), BF16)

    def rows8(ref, base, ex, ey, et, ahead):
        total = jnp.zeros((8, 128), F32)
        for ez in range(3):
            value = jnp.broadcast_to(ref[base(at(ex, ey, ez, et)), :], (8, 128))
            total = jnp.where(zone == (spot + ahead * (ez - 1) + 8) % 8, value, total)
        return total

    def row_one(off):
        return slice(off, off + 1)

    def row_three(o):
        return lambda off: slice(off * 2 + o, off * 2 + o + 1)

    for et in range(3):
        w1_ref[et * 128 + 72 : et * 128 + 128, :] = jnp.zeros((56, 128), BF16)
        for ey in range(3):
            block = [rows8(one, row_one, 2 - turned, ey, et, -1) for turned in range(3)]
            w1_ref[et * 128 + ey * 24 : et * 128 + ey * 24 + 24, :] = jnp.concatenate(block, axis=0).astype(BF16)
        for o in range(2):
            base = (et * 2 + o) * 128
            w3t_ref[base + 72 : base + 128, :] = jnp.zeros((56, 128), BF16)
            for dy in range(3):
                block = [rows8(three, row_three(o), turned, 2 - dy, 2 - et, 1) for turned in range(3)]
                w3t_ref[base + dy * 24 : base + dy * 24 + 24, :] = jnp.concatenate(block, axis=0).astype(BF16)
        for ex in range(3):
            block = []
            for ey in range(3):
                for o in range(2):
                    block.append(rows8(three, row_three(o), ex, ey, et, 1))
            block.append(jnp.zeros((80, 128), F32))
            rows = slice((et * 3 + ex) * 128, (et * 3 + ex) * 128 + 128)
            w3_ref[rows, :] = jnp.concatenate(block, axis=0).T.astype(BF16)
            block = [rows8(one, row_one, 2 - ex, 2 - dy, 2 - et, -1) for dy in range(3)]
            block.append(jnp.zeros((104, 128), F32))
            w1t_ref[rows, :] = jnp.concatenate(block, axis=0).T.astype(BF16)
            for ey in range(3):
                parts = [two[at(ex, ey, ez, et) * 16 : at(ex, ey, ez, et) * 16 + 16, :] for ez in range(3)]
                block = []
                for z in range(8):
                    total = jnp.zeros((16, 128), F32)
                    for ez in range(3):
                        total = jnp.where(wide == (z + ez - 1) % 8, parts[ez], total)
                    block.append(total)
                block = jnp.concatenate(block, axis=0)
                turned = block.T.astype(BF16)
                block = block.astype(BF16)
                for member in range(2):
                    lanes = slice(member * 128, member * 128 + 128)
                    base = ((et * 4 + ey + member) * 3 + ex) * 128
                    w2_ref[base : base + 128, lanes] = turned
                    base = (((2 - et) * 4 + 2 - ey + member) * 3 + 2 - ex) * 128
                    w2t_ref[base : base + 128, lanes] = block
            for member in range(2):
                lanes = slice(member * 128, member * 128 + 128)
                base = ((et * 4 + 3 * (1 - member)) * 3 + ex) * 128
                w2_ref[base : base + 128, lanes] = zeros
                w2t_ref[base : base + 128, lanes] = zeros
    bias_ref[0:1, :] = jnp.concatenate([b1_ref[...]] * 8, axis=1)
    bias_ref[1:2, :] = jnp.concatenate([b2_ref[...]] * 8, axis=1)
    bias_ref[2:3, :] = jnp.broadcast_to(b3_ref[0:1, 0:1], (1, 128))
    bias_ref[3:4, :] = jnp.broadcast_to(b3_ref[0:1, 1:2], (1, 128))
    lane = lax.broadcasted_iota(jnp.int32, (512, 512), 1)
    source = (lane // 4 % 2 * 8 + lane // 16 % 8) * 32 + lane // 8 % 2 * 16 + lane // 128 * 4 + lane % 4
    row = lax.broadcasted_iota(jnp.int32, (512, 512), 0)
    perm_ref[...] = jnp.where(row == source, 1.0, 0.0).astype(BF16)


def split_dot(values, matrix, parts, transposed=False):
    dims = (((1,), (1 if transposed else 0,)), ((), ()))
    total = None
    rest = values
    for _ in range(parts):
        head = rest.astype(BF16)
        rest = rest - head.astype(F32)
        term = lax.dot_general(head, matrix, dims, preferred_element_type=F32)
        total = term if total is None else total + term
    return total


def reverse_matrix():
    source = lax.broadcasted_iota(jnp.int32, (128, 128), 0)
    target = lax.broadcasted_iota(jnp.int32, (128, 128), 1)
    return jnp.where(source == (15 - target // 8) * 8 + target % 8, 1.0, 0.0).astype(BF16)


def spread_rows(values):
    count = values.shape[0] - 2
    site = lax.broadcasted_iota(jnp.int32, (count, 16, 128), 1)
    lane = (lax.broadcasted_iota(jnp.int32, (count, 16, 128), 2) + 8 * site) % 128
    pieces = []
    for second in range(3):
        turned = pltpu.roll(values, 16 + 24 * second, 1)[second : second + count]
        pieces.append(jnp.broadcast_to(turned[:, None, :], (count, 16, 128)))
    wide = jnp.where(lane < 24, pieces[0], jnp.where(lane < 48, pieces[1], pieces[2]))
    return pltpu.roll(wide, 0, 2, stride=8, stride_axis=1)


def gather_rows(values, place):
    count = values.shape[0]
    site = lax.broadcasted_iota(jnp.int32, (count, 16, 128), 1)
    lane = lax.broadcasted_iota(jnp.int32, (count, 16, 128), 2) // 8
    moved = pltpu.roll(values, 0, 2, stride=8, stride_axis=1)
    results = []
    for spot in range(place):
        total = jnp.sum(jnp.where(lane == (site + spot) % 16, moved, 0.0), axis=1)
        results.append(total if spot == 0 else pltpu.roll(total, 128 - 8 * spot, 1))
    return results


def shifted(values):
    return (
        pltpu.roll(values, 1, 1).astype(BF16),
        values.astype(BF16),
        pltpu.roll(values, 15, 1).astype(BF16),
    )


def pair_dot(ref, time, steps, pairs, w_ref):
    total = None
    for first in range(3):
        for start in range(2):
            sides = []
            for block in (2 * start, 2 * start + 1):
                rows = ref[pl.ds(time + first, steps), block // 2 : block // 2 + pairs, block % 2]
                sides.append(rows.reshape(steps * pairs * 16, 384))
            at = (first * 2 + start) * 768
            term = jnp.dot(
                jnp.concatenate(sides, axis=1), w_ref[at : at + 768, :], preferred_element_type=F32
            )
            total = term if total is None else total + term
    return total


def time_dot(ref, time, rows, w_ref):
    sides = [ref[time + first].reshape(rows, ref.shape[-1]) for first in range(3)]
    return jnp.dot(jnp.concatenate(sides, axis=1), w_ref[...], preferred_element_type=F32)


def fold_group(values):
    lane = lax.broadcasted_iota(jnp.int32, values.shape, 1)
    for step in (1, 2, 4):
        down = pltpu.roll(values, 128 - step, 1)
        up = pltpu.roll(values, step, 1)
        values = values + jnp.where((lane // step) % 2 == 0, down, up)
    return values


def main_kernel(
    low_ref, own_ref, high_ref, perm_ref, w1_ref, w3t_ref, w2_ref, w2t_ref, w3_ref, bias_ref,
    out_ref, cot1, held,
    gather, dense_f, dense_m, dense_z, frozen, frozen_x, act1, act2, pre0, pre1, flow, scale_c, shift_c,
    direct, third_x, cot2,
):
    def repeat(count, body):
        for step in range(count):
            body(step)

    for block, ref in enumerate((own_ref, low_ref, high_ref)):
        block = (1, 0, 2)[block]
        for source in range(32):
            spot, half = source // 2, source % 2
            lanes = slice(spot * 32, spot * 32 + 32)
            tile = ref[source].astype(F32)
            for kind in range(3):
                place = kind * 6 + block * 2 + half
                gather[place, 0:16, lanes] = tile[:, 32 * kind : 32 * kind + 32]
                gather[place, 16:18, lanes] = tile[2 * kind : 2 * kind + 2, 96:128]
    ordered = jnp.dot(
        gather[...].reshape(432, 512).astype(BF16), perm_ref[...], preferred_element_type=F32
    )
    for block in range(6):
        head = ordered[block * 24 : block * 24 + 18]
        rest = ordered[144 + block * 24 : 144 + block * 24 + 18]
        share = ordered[288 + block * 24 : 288 + block * 24 + 18]
        for y in range(4):
            lanes = slice(y * 128, y * 128 + 128)
            rows = pl.ds(block * 4 + y, 18, stride=24)
            dense_f[rows, :] = head[:, lanes] + rest[:, lanes]
            dense_m[rows, :] = share[:, lanes]
            dense_z[rows, :] = head[:, lanes] * share[:, lanes]
    reverse = reverse_matrix()
    frozen[...] = jnp.dot(dense_z[...].astype(BF16), reverse, preferred_element_type=F32)

    def spread_frozen(time):
        rows = slice(time * 24, time * 24 + 24)
        frozen_x[time] = spread_rows(frozen[rows, :][1:23]).astype(BF16)

    repeat(18, spread_frozen)


    def first_layer(time):
        total = time_dot(frozen_x, time, 320, w1_ref) + bias_ref[0:1, :]
        for third, part in enumerate(shifted(jnp.tanh(total).reshape(20, 16, 128))):
            act1[time, :, :, :, third * 128 : third * 128 + 128] = part.reshape(10, 2, 16, 128)

    repeat(16, first_layer)


    def second_layer(step):
        total = pair_dot(act1, step * 1, 1, 9, w2_ref)
        for member in range(2):
            values = jnp.tanh(total[:, member * 128 : member * 128 + 128] + bias_ref[1:2, :])
            for third, part in enumerate(shifted(values.reshape(9, 16, 128))):
                act2[pl.ds(step * 1, 1), :, member, :, third * 128 : third * 128 + 128] = part.reshape(1, 9, 16, 128)

    repeat(14, second_layer)


    def third_layer(time):
        total = time_dot(act2, time, 288, w3_ref).reshape(18, 16, 128)
        total = total[0:16] + pltpu.roll(total[1:17], 112, 2) + pltpu.roll(total[2:18], 96, 2)
        scale, shift = gather_rows(total, 2)
        pre0[time] = scale + bias_ref[2:3, :]
        pre1[time] = shift + bias_ref[3:4, :]

    repeat(12, third_layer)

    def transform(time):
        rows = slice((time + 3) * 24, (time + 3) * 24 + 24)
        field = dense_f[rows, :][4:20]
        share = dense_m[rows, :][4:20]
        growth = jnp.exp(jnp.tanh(pre0[time]))
        flow[time] = share * field + (1.0 - share) * (field * growth + pre1[time])

    repeat(12, transform)

    def force_step(time):
        rows = slice((time + 4) * 24, (time + 4) * 24 + 24)
        field = dense_f[rows, :][5:19]
        share = dense_m[rows, :][5:19]
        here = flow[time + 1]
        lane = lax.broadcasted_iota(jnp.int32, (16, 128), 1) % 8
        around = flow[time] + flow[time + 2] + pltpu.roll(here, 8, 1) + pltpu.roll(here, 120, 1)
        around = around + jnp.where(lane == 0, pltpu.roll(here, 121, 1), pltpu.roll(here, 1, 1))
        around = around + jnp.where(lane == 7, pltpu.roll(here, 7, 1), pltpu.roll(here, 127, 1))
        around = around[1:15] + here[0:14] + here[2:16]
        mid = here[1:15]
        force = -0.5 * around + 1.8 * mid + 0.2 * mid * mid * mid
        scale = jnp.tanh(pre0[time + 1][1:15])
        growth = jnp.exp(scale)
        active = 1.0 - share
        empty = jnp.zeros((2, 128), F32)
        scale_c[time] = jnp.concatenate(
            [active * (force * field * growth - 1.0) * (1.0 - scale * scale), empty], axis=0
        )
        shift_c[time] = jnp.concatenate([active * force, empty], axis=0)
        direct[time] = force * (share + active * growth)

    repeat(10, force_step)
    scale_c[...] = jnp.dot(
        scale_c[...].reshape(160, 128).astype(BF16), reverse, preferred_element_type=F32
    ).reshape(10, 16, 128)
    shift_c[...] = jnp.dot(
        shift_c[...].reshape(160, 128).astype(BF16), reverse, preferred_element_type=F32
    ).reshape(10, 16, 128)

    def spread_third(time):
        third_x[time, :, :, 0:128] = spread_rows(scale_c[time][0:14]).astype(BF16)
        third_x[time, :, :, 128:256] = spread_rows(shift_c[time][0:14]).astype(BF16)

    repeat(10, spread_third)


    def second_cot(time):
        total = time_dot(third_x, time, 192, w3t_ref)
        act = act2[time + 3, :, :, :, 128:256].reshape(18, 16, 128)[3:15].astype(F32)
        values = total.reshape(12, 16, 128) * (1.0 - act * act)
        for third, part in enumerate(shifted(values)):
            cot2[time, :, :, :, third * 128 : third * 128 + 128] = part.reshape(6, 2, 16, 128)

    repeat(8, second_cot)


    def first_cot(step):
        total = pair_dot(cot2, step * 3, 3, 5, w2t_ref)
        for member in range(2):
            act = act1[pl.ds(step * 3 + 5, 3), 2 + member : 7 + member, 1 - member, :, 128:256]
            act = act.astype(F32).reshape(15, 16, 128)
            values = total[:, member * 128 : member * 128 + 128].reshape(15, 16, 128) * (1.0 - act * act)
            for third, part in enumerate(shifted(values)):
                cot1[pl.ds(step * 3, 3), :, member, :, third * 128 : third * 128 + 128] = part.reshape(3, 5, 16, 128)

    repeat(2, first_cot)

    for time in range(4):
        rows = slice(time * 8, time * 8 + 8)
        held[0, rows, :] = flow[time + 4][4:12]
        held[1, rows, :] = direct[time + 3][3:11]
        held[2, rows, :] = dense_m[(time + 7) * 24 + 8 : (time + 7) * 24 + 16, :]

    def put(block, values):
        out_ref[2 * block, :, :] = values[0:8]
        out_ref[2 * block + 1, :, :] = values[8:16]

    own2 = cot2[2:6, 1:5, :, :, 128:256].reshape(512, 128).astype(F32)
    own1 = cot1[1:5, :, :, :, 128:256].reshape(4, 10, 16, 128)[:, 1:9].reshape(512, 128).astype(F32)
    own_a = act2[5:9, :, :, :, 128:256].reshape(4, 18, 16, 128)[:, 5:13].reshape(512, 128).astype(F32)
    turn2 = own2.T.astype(BF16)
    turn1 = own1.T.astype(BF16)
    turn_a = own_a.T.astype(BF16)
    zone = lax.broadcasted_iota(jnp.int32, (16, 128), 1)

    def lane_sum(values, lanes_zone, shift):
        total = jnp.zeros((16, 128), F32)
        for z in range(8):
            total = total + jnp.where(lanes_zone == (z + shift) % 8, values[z * 16 : z * 16 + 16], 0.0)
        return total

    packed = [None] * 11
    for first in range(3):
        for second in range(3):
            low = (5 + second) // 2
            block = act1[5 + first : 9 + first, low : low + 5].reshape(4, 10, 16, 384)
            start = 5 + second - 2 * low
            block = block[:, start : start + 8].reshape(512, 384)
            product = jnp.dot(turn2, block, preferred_element_type=F32)
            for third in range(3):
                for ez in range(3):
                    number = ((third * 3 + second) * 3 + ez) * 3 + first
                    part = lane_sum(product[:, third * 128 : third * 128 + 128], zone // 16, ez - 1)
                    for step in (64, 32, 16):
                        part = part + pltpu.roll(part, step, 1)
                    old = packed[number // 8]
                    packed[number // 8] = (
                        part if old is None else jnp.where(zone // 16 == number % 8, part, old)
                    )
    for number in range(11):
        put(number, packed[number])

    extra = jnp.zeros((16, 128), F32)
    for first in range(3):
        block = third_x[2 + first : 6 + first, 2:10].reshape(512, 256)
        product = jnp.dot(turn_a, block, preferred_element_type=F32)
        total = jnp.zeros((16, 128), F32)
        for o in range(2):
            for ez in range(3):
                part = fold_group(lane_sum(product[:, o * 128 : o * 128 + 128], zone % 8, 1 - ez))
                total = jnp.where(zone % 8 == o * 3 + ez, part, total)
        block = frozen_x[6 + first : 10 + first, 6:14].reshape(512, 128)
        product = jnp.dot(turn1, block, preferred_element_type=F32)
        for ez in range(3):
            part = fold_group(lane_sum(product, zone % 8, ez - 1))
            if ez < 2:
                total = jnp.where(zone % 8 == 6 + ez, part, total)
            else:
                extra = jnp.where(zone % 8 == first, part, extra)
        put(11 + first, total)
    put(14, extra)
    sums = [
        jnp.sum(own1, axis=0, keepdims=True),
        jnp.sum(own2, axis=0, keepdims=True),
        jnp.sum(jnp.sum(scale_c[3:7], axis=0)[3:11], axis=0, keepdims=True),
        jnp.sum(jnp.sum(shift_c[3:7], axis=0)[3:11], axis=0, keepdims=True),
    ]
    site = lax.broadcasted_iota(jnp.int32, (16, 128), 0)
    total = jnp.zeros((16, 128), F32)
    for row, value in enumerate(sums):
        total = jnp.where(site == row, jnp.broadcast_to(value, (16, 128)), total)
    put(15, total)


def input_grad_kernel(cot1_ref, held_ref, w1t_ref, perm_ref, out_ref, own_out, rows_out):
    for time in range(4):
        total = time_dot(cot1_ref, time, 160, w1t_ref).reshape(10, 16, 128)
        total = total[0:8] + pltpu.roll(total[1:9], 120, 2) + pltpu.roll(total[2:10], 112, 2)
        (total,) = gather_rows(total, 1)
        rows = slice(time * 8, time * 8 + 8)
        own_out[rows, :] = held_ref[0, rows, :]
        own_out[32 + time * 8 : 40 + time * 8, :] = held_ref[1, rows, :] + held_ref[2, rows, :] * total
    for kind in range(2):
        for half in range(2):
            for y in range(4):
                rows_out[(kind * 2 + half) * 4 : (kind * 2 + half) * 4 + 4, y * 128 : y * 128 + 128] = own_out[
                    pl.ds(kind * 32 + half * 4 + y, 4, stride=8), :
                ]
    ordered = split_dot(rows_out[...], perm_ref[...], 3, transposed=True)
    for target in range(32):
        spot, half = target // 2, target % 2
        lanes = slice(spot * 32, spot * 32 + 32)
        out_ref[target] = jnp.zeros((8, 128), F32)
        out_ref[target, 0:4, 0:32] = ordered[half * 4 : half * 4 + 4, lanes]
        out_ref[target, 0:4, 32:64] = ordered[8 + half * 4 : 12 + half * 4, lanes]


def unpack_kernel(in_ref, flowed_ref, grad_ref, g1_ref, g2_ref, g3_ref, b1_ref, b2_ref, b3_ref, window, extra, turned_x):
    for source in range(32):
        window[4 * source : 4 * source + 4, :] = in_ref[source, 8:12, :]
    turned = window[...].T
    flowed_ref[...] = turned[0:32]
    grad_ref[...] = turned[32:64]

    def group(number):
        return jnp.concatenate([in_ref[2 * number, 0:8, :], in_ref[2 * number + 1, 0:8, :]], axis=0)

    for number in range(11):
        block = group(number)
        for slot in range(min(8, 81 - number * 8)):
            g2_ref[number * 8 + slot] = block[:, slot * 16 : slot * 16 + 16]
    for number in range(4):
        extra[number * 16 : number * 16 + 16, :] = group(11 + number)
    extra[64:128, :] = jnp.zeros((64, 128), F32)
    turned_x[...] = extra[...].T
    for et in range(3):
        lanes = slice(et * 16, et * 16 + 16)
        for ey in range(3):
            for ex in range(3):
                for ez in range(3):
                    off = ((ex * 3 + ey) * 3 + ez) * 3
                    row = ey * 24 + (2 - ex) * 8
                    if ez < 2:
                        g1_ref[off + et] = turned_x[row + 6 + ez : row + 7 + ez, lanes]
                    else:
                        g1_ref[off + et] = turned_x[row + et : row + et + 1, 48:64]
                    row = (2 - ey) * 24 + ex * 8 + ez
                    g3_ref[off + 2 - et, 0:1, :] = turned_x[row : row + 1, lanes]
                    g3_ref[off + 2 - et, 1:2, :] = turned_x[row + 3 : row + 4, lanes]
    sums = in_ref[30, 0:8, :]
    lane = lax.broadcasted_iota(jnp.int32, (1, 128), 1)
    total = jnp.sum(sums, axis=1, keepdims=True)
    b3_ref[...] = jnp.where(lane == 0, total[2:3], total[3:4])[:, 0:2]
    for step in (64, 32, 16):
        sums = sums + pltpu.roll(sums, step, 1)
    b1_ref[...] = sums[0:1, 0:16]
    b2_ref[...] = sums[1:2, 0:16]


def ring(count, step):
    return [(i, (i + step) % count) for i in range(count)]


def shape(dims, dtype=F32):
    return jax.ShapeDtypeStruct(dims, dtype)


def run_weights(kernel_one, bias_one, kernel_two, bias_two, kernel_three, bias_three):
    return pl.pallas_call(
        weights_kernel,
        out_shape=[
            shape((384, 128), BF16),
            shape((768, 128), BF16),
            shape((4608, 256), BF16),
            shape((4608, 256), BF16),
            shape((1152, 128), BF16),
            shape((1152, 128), BF16),
            shape((4, 128)),
            shape((512, 512), BF16),
        ],
        in_specs=[VMEM_SPEC] * 6,
        out_specs=[VMEM_SPEC] * 8,
        scratch_shapes=[
            pltpu.VMEM((81, 128), F32),
            pltpu.VMEM((1296, 128), F32),
            pltpu.VMEM((162, 128), F32),
        ],
        compiler_params=pltpu.CompilerParams(vmem_limit_bytes=12 * 2**20),
        cost_estimate=pl.CostEstimate(flops=10**6, bytes_accessed=8 * 10**6, transcendentals=0),
        name="weights",
    )(
        kernel_one[:, 0].transpose(1, 2, 3, 4, 0).reshape(81, 16),
        kernel_two.transpose(2, 3, 4, 5, 0, 1).reshape(1296, 16),
        kernel_three.transpose(2, 3, 4, 5, 0, 1).reshape(162, 16),
        bias_one.reshape(1, 16),
        bias_two.reshape(1, 16),
        bias_three.reshape(1, 2),
    )


def run_main(*operands, name="flow"):
    return pl.pallas_call(
        main_kernel,
        out_shape=[
            shape((32, 8, 128)),
            shape((6, 5, 2, 16, 384), BF16),
            shape((3, 32, 128)),
        ],
        in_specs=[VMEM_SPEC] * 10,
        out_specs=[VMEM_SPEC] * 3,
        scratch_shapes=[
            pltpu.VMEM((18, 24, 512), F32),
            pltpu.VMEM((432, 128), F32),
            pltpu.VMEM((432, 128), F32),
            pltpu.VMEM((432, 128), F32),
            pltpu.VMEM((432, 128), F32),
            pltpu.VMEM((18, 20, 16, 128), BF16),
            pltpu.VMEM((16, 10, 2, 16, 384), BF16),
            pltpu.VMEM((14, 9, 2, 16, 384), BF16),
            pltpu.VMEM((12, 16, 128), F32),
            pltpu.VMEM((12, 16, 128), F32),
            pltpu.VMEM((12, 16, 128), F32),
            pltpu.VMEM((10, 16, 128), F32),
            pltpu.VMEM((10, 16, 128), F32),
            pltpu.VMEM((10, 14, 128), F32),
            pltpu.VMEM((10, 12, 16, 256), BF16),
            pltpu.VMEM((8, 6, 2, 16, 384), BF16),
        ],
        compiler_params=pltpu.CompilerParams(vmem_limit_bytes=28 * 2**20),
        cost_estimate=pl.CostEstimate(flops=2 * 10**10, bytes_accessed=8 * 10**6, transcendentals=10**6),
        name=name,
    )(*operands)


def main_shapes():
    return [
        shape((32, 16, 128), BF16), shape((32, 16, 128), BF16), shape((32, 16, 128), BF16), shape((512, 512), BF16), shape((384, 128), BF16), shape((768, 128), BF16),
        shape((4608, 256), BF16), shape((4608, 256), BF16), shape((1152, 128), BF16), shape((4, 128)),
    ]


def local(field, parity_mask, kernel_one, bias_one, kernel_two, bias_two, kernel_three, bias_three):
    packed = pl.pallas_call(
        pack_kernel,
        out_shape=shape((32, 16, 128), BF16),
        in_specs=[VMEM_SPEC] * 2,
        out_specs=VMEM_SPEC,
        scratch_shapes=[pltpu.VMEM((3, 144, 128), F32)],
        name="pack",
    )(field.reshape(32, 128), parity_mask.reshape(32, 128))
    own = lax.all_to_all(packed, GROUP, 0, 0)
    low = lax.ppermute(own, "gyh", ring(8, 1))
    high = lax.ppermute(own, "gyh", ring(8, -1))
    w1, w3t, w2, w2t, w3, w1t, bias, perm = run_weights(
        kernel_one, bias_one, kernel_two, bias_two, kernel_three, bias_three
    )
    shares, cot1, held = run_main(low, own, high, perm, w1, w3t, w2, w2t, w3, bias)
    shares = lax.all_to_all(shares, GROUP, 0, 0)
    outputs = pl.pallas_call(
        input_grad_kernel,
        out_shape=shape((32, 8, 128)),
        in_specs=[VMEM_SPEC] * 4,
        out_specs=VMEM_SPEC,
        scratch_shapes=[
            pltpu.VMEM((64, 128), F32),
            pltpu.VMEM((16, 512), F32),
        ],
        compiler_params=pltpu.CompilerParams(vmem_limit_bytes=8 * 2**20),
        cost_estimate=pl.CostEstimate(flops=5 * 10**8, bytes_accessed=3 * 10**6, transcendentals=0),
        name="input_grad",
    )(cot1, held, w1t, perm)
    share = jnp.broadcast_to(jnp.sum(shares, axis=0)[None], (8, 8, 128))
    share = lax.all_to_all(share, "gyh", 0, 0)
    share = jnp.sum(share, axis=0) * (1.0 / VOLUME)
    last = jnp.concatenate([jnp.broadcast_to(share[None], (32, 8, 128)), outputs], axis=1)
    last = lax.all_to_all(last, GROUP, 0, 0)
    flowed, field_grad, g1, g2, g3, b1, b2, b3 = pl.pallas_call(
        unpack_kernel,
        out_shape=[
            shape((32, 128)), shape((32, 128)), shape((81, 1, 16)), shape((81, 16, 16)), shape((81, 2, 16)),
            shape((1, 16)), shape((1, 16)), shape((1, 2)),
        ],
        in_specs=[VMEM_SPEC],
        out_specs=[VMEM_SPEC] * 8,
        scratch_shapes=[pltpu.VMEM((128, 128), F32), pltpu.VMEM((128, 128), F32), pltpu.VMEM((128, 128), F32)],
        name="unpack",
    )(last)
    return (
        flowed.reshape(2, 4, 4, 128),
        field_grad.reshape(2, 4, 4, 128),
        g1.reshape(3, 3, 3, 3, 1, 16).transpose(5, 4, 0, 1, 2, 3),
        b1.reshape(16),
        g2.reshape(3, 3, 3, 3, 16, 16).transpose(4, 5, 0, 1, 2, 3),
        b2.reshape(16),
        g3.reshape(3, 3, 3, 3, 2, 16).transpose(4, 5, 0, 1, 2, 3),
        b3.reshape(2),
    )


def solution(mesh):
    split = Mesh(mesh.devices.reshape(8, 8, 2, 2), ("gx", "gyh", "gyl", "gz"))
    block = P("gx", ("gyh", "gyl"), "gz", None)
    return jax.shard_map(
        local,
        mesh=split,
        in_specs=(block, block, P(), P(), P(), P(), P(), P()),
        out_specs=(block, block, P(), P(), P(), P(), P(), P()),
        check_vma=False,
    )
```

```python
import functools

import jax
import jax.numpy as jnp
from jax import lax
from jax.experimental import pallas as pl
from jax.experimental.pallas import tpu as pltpu
from jax.sharding import Mesh
from jax.sharding import PartitionSpec as P

F32 = jnp.float32
BF16 = jnp.bfloat16
GROUP = ("gz", "gx", "gyl")
VMEM_SPEC = pl.BlockSpec(memory_space=pltpu.VMEM)
VOLUME = 1048576.0


def pack_kernel(field_ref, mask_ref, out_ref, window):
    field = field_ref[...]
    head = field.astype(BF16).astype(F32)
    empty = jnp.zeros((32, 128), F32)
    both = jnp.concatenate([head, field - head, mask_ref[...].astype(F32)], axis=0)
    near = jnp.concatenate([pltpu.roll(both, 7, 1), empty], axis=0).T
    later = jnp.concatenate([empty, pltpu.roll(both, 119, 1)], axis=0).T
    lane = lax.broadcasted_iota(jnp.int32, (128, 128), 1)
    rows = [near]
    for kind in range(3):
        turned = pltpu.roll(later, 64 - 32 * kind, 1)
        rows.append(jnp.where(lane < 96, near, pltpu.roll(turned, 2 * kind, 0)))
    for number in range(1, 4):
        window[number - 1, 0:128, :] = rows[number]
        window[number - 1, 128:144, :] = rows[number][0:16, :]
    row = lax.broadcasted_iota(jnp.int32, (16, 128), 0)
    for slot in range(32):
        here = slice(4 * slot, 4 * slot + 16)
        out_ref[slot] = jnp.where(
            row < 2, window[0, here, :], jnp.where(row < 4, window[1, here, :], window[2, here, :])
        ).astype(BF16)


def tile_dot(values):
    spot = lax.broadcasted_iota(jnp.int32, (16, 128), 0)
    lane = lax.broadcasted_iota(jnp.int32, (16, 128), 1)
    return jnp.dot(values, jnp.where(lane % 16 == spot, 1.0, 0.0).astype(BF16), preferred_element_type=F32)


def weights_kernel(
    k1_ref, k2_ref, k3_ref, b1_ref, b2_ref, b3_ref,
    w1_ref, w3t_ref, w2_ref, w2t_ref, w3_ref, w1t_ref, bias_ref, perm_ref, one, two, three,
):
    def at(ex, ey, ez, et):
        return ((ex * 3 + ey) * 3 + ez) * 3 + et

    one[0:81, :] = tile_dot(k1_ref[...])
    two[...] = tile_dot(k2_ref[...])
    three[0:162, :] = tile_dot(k3_ref[...])
    zone = lax.broadcasted_iota(jnp.int32, (8, 128), 1) // 16
    spot = lax.broadcasted_iota(jnp.int32, (8, 128), 0)
    wide = lax.broadcasted_iota(jnp.int32, (16, 128), 1) // 16
    zeros = jnp.zeros((128, 128), BF16)

    def rows8(ref, base, ex, ey, et, ahead):
        total = jnp.zeros((8, 128), F32)
        for ez in range(3):
            value = jnp.broadcast_to(ref[base(at(ex, ey, ez, et)), :], (8, 128))
            total = jnp.where(zone == (spot + ahead * (ez - 1) + 8) % 8, value, total)
        return total

    def row_one(off):
        return slice(off, off + 1)

    def row_three(o):
        return lambda off: slice(off * 2 + o, off * 2 + o + 1)

    for et in range(3):
        block = []
        for ey in range(3):
            block += [rows8(one, row_one, 2 - turned, ey, et, -1) for turned in range(3)]
        block.append(jnp.zeros((56, 128), F32))
        w1_ref[et * 128 : et * 128 + 128, :] = jnp.concatenate(block, axis=0).astype(BF16)
        for o in range(2):
            base = (et * 2 + o) * 128
            block = []
            for dy in range(3):
                block += [rows8(three, row_three(o), turned, 2 - dy, 2 - et, 1) for turned in range(3)]
            block.append(jnp.zeros((56, 128), F32))
            w3t_ref[base : base + 128, :] = jnp.concatenate(block, axis=0).astype(BF16)
        for ex in range(3):
            block = []
            for ey in range(3):
                for o in range(2):
                    block.append(rows8(three, row_three(o), ex, ey, et, 1))
            block.append(jnp.zeros((80, 128), F32))
            rows = slice((et * 3 + ex) * 128, (et * 3 + ex) * 128 + 128)
            w3_ref[rows, :] = jnp.concatenate(block, axis=0).T.astype(BF16)
            block = [rows8(one, row_one, 2 - ex, 2 - dy, 2 - et, -1) for dy in range(3)]
            block.append(jnp.zeros((104, 128), F32))
            w1t_ref[rows, :] = jnp.concatenate(block, axis=0).T.astype(BF16)
            for ey in range(3):
                parts = [two[at(ex, ey, ez, et) * 16 : at(ex, ey, ez, et) * 16 + 16, :] for ez in range(3)]
                block = []
                for z in range(8):
                    total = jnp.zeros((16, 128), F32)
                    for ez in range(3):
                        total = jnp.where(wide == (z + ez - 1) % 8, parts[ez], total)
                    block.append(total)
                block = jnp.concatenate(block, axis=0)
                turned = block.T.astype(BF16)
                block = block.astype(BF16)
                for member in range(2):
                    lanes = slice(member * 128, member * 128 + 128)
                    base = ((et * 4 + ey + member) * 3 + ex) * 128
                    w2_ref[base : base + 128, lanes] = turned
                    base = (((2 - et) * 4 + 2 - ey + member) * 3 + 2 - ex) * 128
                    w2t_ref[base : base + 128, lanes] = block
            for member in range(2):
                lanes = slice(member * 128, member * 128 + 128)
                base = ((et * 4 + 3 * (1 - member)) * 3 + ex) * 128
                w2_ref[base : base + 128, lanes] = zeros
                w2t_ref[base : base + 128, lanes] = zeros
    bias_ref[...] = jnp.concatenate(
        [
            jnp.concatenate([b1_ref[...]] * 8, axis=1),
            jnp.concatenate([b2_ref[...]] * 8, axis=1),
            jnp.broadcast_to(b3_ref[0:1, 0:1], (1, 128)),
            jnp.broadcast_to(b3_ref[0:1, 1:2], (1, 128)),
            jnp.zeros((4, 128), F32),
        ],
        axis=0,
    )
    lane = lax.broadcasted_iota(jnp.int32, (512, 512), 1)
    source = (lane // 4 % 2 * 8 + lane // 16 % 8) * 32 + lane // 8 % 2 * 16 + lane // 128 * 4 + lane % 4
    row = lax.broadcasted_iota(jnp.int32, (512, 512), 0)
    perm_ref[...] = jnp.where(row == source, 1.0, 0.0).astype(BF16)


def split_dot(values, matrix, parts, transposed=False):
    dims = (((1,), (1 if transposed else 0,)), ((), ()))
    total = None
    rest = values
    for _ in range(parts):
        head = rest.astype(BF16)
        rest = rest - head.astype(F32)
        term = lax.dot_general(head, matrix, dims, preferred_element_type=F32)
        total = term if total is None else total + term
    return total


def reverse_matrix():
    source = lax.broadcasted_iota(jnp.int32, (128, 128), 0)
    target = lax.broadcasted_iota(jnp.int32, (128, 128), 1)
    return jnp.where(source == (15 - target // 8) * 8 + target % 8, 1.0, 0.0).astype(BF16)


def spread_rows(values):
    count = values.shape[0] - 2
    site = lax.broadcasted_iota(jnp.int32, (count, 16, 128), 1)
    lane = (lax.broadcasted_iota(jnp.int32, (count, 16, 128), 2) + 8 * site) % 128
    pieces = []
    for second in range(3):
        turned = pltpu.roll(values, 16 + 24 * second, 1)[second : second + count]
        pieces.append(jnp.broadcast_to(turned[:, None, :], (count, 16, 128)))
    wide = jnp.where(lane < 24, pieces[0], jnp.where(lane < 48, pieces[1], pieces[2]))
    return pltpu.roll(wide, 0, 2, stride=8, stride_axis=1)


def gather_rows(values, place):
    count = values.shape[0]
    site = lax.broadcasted_iota(jnp.int32, (count, 16, 128), 1)
    lane = lax.broadcasted_iota(jnp.int32, (count, 16, 128), 2) // 8
    moved = pltpu.roll(values, 0, 2, stride=8, stride_axis=1)
    results = []
    for spot in range(place):
        total = jnp.sum(jnp.where(lane == (site + spot) % 16, moved, 0.0), axis=1)
        results.append(total if spot == 0 else pltpu.roll(total, 128 - 8 * spot, 1))
    return results


def shifted(values):
    return (
        pltpu.roll(values, 1, 1).astype(BF16),
        values.astype(BF16),
        pltpu.roll(values, 15, 1).astype(BF16),
    )


def pair_dot(ref, time, steps, pairs, w_ref):
    total = None
    for first in range(3):
        for start in range(2):
            sides = []
            for block in (2 * start, 2 * start + 1):
                rows = ref[pl.ds(time + first, steps), block // 2 : block // 2 + pairs, block % 2]
                sides.append(rows.reshape(steps * pairs * 16, 384))
            at = (first * 2 + start) * 768
            term = jnp.dot(
                jnp.concatenate(sides, axis=1), w_ref[at : at + 768, :], preferred_element_type=F32
            )
            total = term if total is None else total + term
    return total


def time_dot(ref, time, rows, w_ref):
    sides = [ref[time + first].reshape(rows, ref.shape[-1]) for first in range(3)]
    return jnp.dot(jnp.concatenate(sides, axis=1), w_ref[...], preferred_element_type=F32)


def fold_group(values):
    lane = lax.broadcasted_iota(jnp.int32, values.shape, 1)
    for step in (1, 2, 4):
        down = pltpu.roll(values, 128 - step, 1)
        up = pltpu.roll(values, step, 1)
        values = values + jnp.where((lane // step) % 2 == 0, down, up)
    return values


def main_kernel(
    low_ref, own_ref, high_ref, perm_ref, w1_ref, w3t_ref, w2_ref, w2t_ref, w3_ref, bias_ref,
    out_ref, cot1, held,
    gather, dense_f, dense_m, dense_z, frozen, frozen_x, act1, act2, pre0, pre1, flow, scale_c, shift_c,
    direct, third_x, cot2,
):
    def repeat(count, body):
        for step in range(count):
            body(step)

    for block, ref in enumerate((own_ref, low_ref, high_ref)):
        block = (1, 0, 2)[block]
        for source in range(32):
            spot, half = source // 2, source % 2
            lanes = slice(spot * 32, spot * 32 + 32)
            tile = ref[source].astype(F32)
            for kind in range(3):
                place = kind * 6 + block * 2 + half
                gather[place, 0:16, lanes] = tile[:, 32 * kind : 32 * kind + 32]
                gather[place, 16:18, lanes] = tile[2 * kind : 2 * kind + 2, 96:128]
    ordered = jnp.dot(
        gather[...].reshape(432, 512).astype(BF16), perm_ref[...], preferred_element_type=F32
    )
    for block in range(6):
        head = ordered[block * 24 : block * 24 + 18]
        rest = ordered[144 + block * 24 : 144 + block * 24 + 18]
        share = ordered[288 + block * 24 : 288 + block * 24 + 18]
        for y in range(4):
            lanes = slice(y * 128, y * 128 + 128)
            rows = pl.ds(block * 4 + y, 18, stride=24)
            dense_f[rows, :] = head[:, lanes] + rest[:, lanes]
            dense_m[rows, :] = share[:, lanes]
            dense_z[rows, :] = head[:, lanes] * share[:, lanes]
    reverse = reverse_matrix()
    frozen[...] = jnp.dot(dense_z[0:432, :].astype(BF16), reverse, preferred_element_type=F32)

    def spread_frozen(time):
        rows = slice(time * 24, time * 24 + 24)
        frozen_x[time] = spread_rows(frozen[rows, :][1:23]).astype(BF16)

    repeat(18, spread_frozen)


    def first_layer(time):
        total = time_dot(frozen_x, time, 320, w1_ref) + bias_ref[0:1, :]
        for third, part in enumerate(shifted(jnp.tanh(total).reshape(20, 16, 128))):
            act1[time, :, :, :, third * 128 : third * 128 + 128] = part.reshape(10, 2, 16, 128)

    repeat(16, first_layer)


    def second_layer(step):
        total = pair_dot(act1, step * 1, 1, 9, w2_ref)
        for member in range(2):
            values = jnp.tanh(total[:, member * 128 : member * 128 + 128] + bias_ref[1:2, :])
            for third, part in enumerate(shifted(values.reshape(9, 16, 128))):
                act2[pl.ds(step * 1, 1), :, member, :, third * 128 : third * 128 + 128] = part.reshape(1, 9, 16, 128)

    repeat(14, second_layer)


    def third_layer(time):
        total = time_dot(act2, time, 288, w3_ref).reshape(18, 16, 128)
        total = total[0:16] + pltpu.roll(total[1:17], 112, 2) + pltpu.roll(total[2:18], 96, 2)
        scale, shift = gather_rows(total, 2)
        pre0[time] = scale + bias_ref[2:3, :]
        pre1[time] = shift + bias_ref[3:4, :]

    repeat(12, third_layer)

    def transform(time):
        rows = slice((time + 3) * 24, (time + 3) * 24 + 24)
        field = dense_f[rows, :][4:20]
        share = dense_m[rows, :][4:20]
        growth = jnp.exp(jnp.tanh(pre0[time]))
        flow[time] = share * field + (1.0 - share) * (field * growth + pre1[time])

    repeat(12, transform)

    def force_step(time):
        rows = slice((time + 4) * 24, (time + 4) * 24 + 24)
        field = dense_f[rows, :][5:19]
        share = dense_m[rows, :][5:19]
        here = flow[time + 1]
        lane = lax.broadcasted_iota(jnp.int32, (16, 128), 1) % 8
        around = flow[time] + flow[time + 2] + pltpu.roll(here, 8, 1) + pltpu.roll(here, 120, 1)
        around = around + jnp.where(lane == 0, pltpu.roll(here, 121, 1), pltpu.roll(here, 1, 1))
        around = around + jnp.where(lane == 7, pltpu.roll(here, 7, 1), pltpu.roll(here, 127, 1))
        around = around[1:15] + here[0:14] + here[2:16]
        mid = here[1:15]
        force = -0.5 * around + 1.8 * mid + 0.2 * mid * mid * mid
        scale = jnp.tanh(pre0[time + 1][1:15])
        growth = jnp.exp(scale)
        active = 1.0 - share
        empty = jnp.zeros((2, 128), F32)
        scale_c[time] = jnp.concatenate(
            [active * (force * field * growth - 1.0) * (1.0 - scale * scale), empty], axis=0
        )
        shift_c[time] = jnp.concatenate([active * force, empty], axis=0)
        direct[time] = jnp.concatenate([force * (share + active * growth), empty], axis=0)

    repeat(10, force_step)
    scale_c[...] = jnp.dot(
        scale_c[...].reshape(160, 128).astype(BF16), reverse, preferred_element_type=F32
    ).reshape(10, 16, 128)
    shift_c[...] = jnp.dot(
        shift_c[...].reshape(160, 128).astype(BF16), reverse, preferred_element_type=F32
    ).reshape(10, 16, 128)

    def spread_third(time):
        third_x[time, :, :, 0:128] = spread_rows(scale_c[time][0:14]).astype(BF16)
        third_x[time, :, :, 128:256] = spread_rows(shift_c[time][0:14]).astype(BF16)

    repeat(10, spread_third)


    def second_cot(time):
        total = time_dot(third_x, time, 192, w3t_ref)
        act = act2[time + 3, :, :, :, 128:256].reshape(18, 16, 128)[3:15].astype(F32)
        values = total.reshape(12, 16, 128) * (1.0 - act * act)
        for third, part in enumerate(shifted(values)):
            cot2[time, :, :, :, third * 128 : third * 128 + 128] = part.reshape(6, 2, 16, 128)

    repeat(8, second_cot)


    def first_cot(step):
        total = pair_dot(cot2, step * 3, 3, 5, w2t_ref)
        for member in range(2):
            act = act1[pl.ds(step * 3 + 5, 3), 2 + member : 7 + member, 1 - member, :, 128:256]
            act = act.astype(F32).reshape(15, 16, 128)
            values = total[:, member * 128 : member * 128 + 128].reshape(15, 16, 128) * (1.0 - act * act)
            for third, part in enumerate(shifted(values)):
                cot1[pl.ds(step * 3, 3), :, member, :, third * 128 : third * 128 + 128] = part.reshape(3, 5, 16, 128)

    repeat(2, first_cot)

    for time in range(4):
        rows = slice(time * 8, time * 8 + 8)
        held[0, rows, :] = flow[time + 4][4:12]
        held[1, rows, :] = direct[time + 3][3:11]
        held[2, rows, :] = dense_m[(time + 7) * 24 + 8 : (time + 7) * 24 + 16, :]

    def put(block, values):
        out_ref[2 * block, :, :] = values[0:8]
        out_ref[2 * block + 1, :, :] = values[8:16]

    own2 = cot2[2:6, 1:5, :, :, 128:256].reshape(512, 128).astype(F32)
    own1 = cot1[1:5, :, :, :, 128:256].reshape(4, 10, 16, 128)[:, 1:9].reshape(512, 128).astype(F32)
    own_a = act2[5:9, :, :, :, 128:256].reshape(4, 18, 16, 128)[:, 5:13].reshape(512, 128).astype(F32)
    turn2 = own2.T.astype(BF16)
    turn1 = own1.T.astype(BF16)
    turn_a = own_a.T.astype(BF16)
    zone = lax.broadcasted_iota(jnp.int32, (16, 128), 1)

    def lane_sum(values, lanes_zone, shift):
        total = jnp.zeros((16, 128), F32)
        for z in range(8):
            total = total + jnp.where(lanes_zone == (z + shift) % 8, values[z * 16 : z * 16 + 16], 0.0)
        return total

    packed = [None] * 11
    for first in range(3):
        for second in range(3):
            low = (5 + second) // 2
            block = act1[5 + first : 9 + first, low : low + 5].reshape(4, 10, 16, 384)
            start = 5 + second - 2 * low
            block = block[:, start : start + 8].reshape(512, 384)
            product = jnp.dot(turn2, block, preferred_element_type=F32)
            for third in range(3):
                for ez in range(3):
                    number = ((third * 3 + second) * 3 + ez) * 3 + first
                    part = lane_sum(product[:, third * 128 : third * 128 + 128], zone // 16, ez - 1)
                    for step in (64, 32, 16):
                        part = part + pltpu.roll(part, step, 1)
                    old = packed[number // 8]
                    packed[number // 8] = (
                        part if old is None else jnp.where(zone // 16 == number % 8, part, old)
                    )
    for number in range(11):
        put(number, packed[number])

    extra = jnp.zeros((16, 128), F32)
    for first in range(3):
        block = third_x[2 + first : 6 + first, 2:10].reshape(512, 256)
        product = jnp.dot(turn_a, block, preferred_element_type=F32)
        total = jnp.zeros((16, 128), F32)
        for o in range(2):
            for ez in range(3):
                part = fold_group(lane_sum(product[:, o * 128 : o * 128 + 128], zone % 8, 1 - ez))
                total = jnp.where(zone % 8 == o * 3 + ez, part, total)
        block = frozen_x[6 + first : 10 + first, 6:14].reshape(512, 128)
        product = jnp.dot(turn1, block, preferred_element_type=F32)
        for ez in range(3):
            part = fold_group(lane_sum(product, zone % 8, ez - 1))
            if ez < 2:
                total = jnp.where(zone % 8 == 6 + ez, part, total)
            else:
                extra = jnp.where(zone % 8 == first, part, extra)
        put(11 + first, total)
    put(14, extra)
    sums = [
        jnp.sum(own1, axis=0, keepdims=True),
        jnp.sum(own2, axis=0, keepdims=True),
        jnp.sum(jnp.sum(scale_c[3:7], axis=0)[3:11], axis=0, keepdims=True),
        jnp.sum(jnp.sum(shift_c[3:7], axis=0)[3:11], axis=0, keepdims=True),
    ]
    site = lax.broadcasted_iota(jnp.int32, (16, 128), 0)
    total = jnp.zeros((16, 128), F32)
    for row, value in enumerate(sums):
        total = jnp.where(site == row, jnp.broadcast_to(value, (16, 128)), total)
    put(15, total)


def input_grad_kernel(cot1_ref, held_ref, w1t_ref, perm_ref, out_ref, own_out, rows_out):
    for time in range(4):
        total = time_dot(cot1_ref, time, 160, w1t_ref).reshape(10, 16, 128)
        total = total[0:8] + pltpu.roll(total[1:9], 120, 2) + pltpu.roll(total[2:10], 112, 2)
        (total,) = gather_rows(total, 1)
        rows = slice(time * 8, time * 8 + 8)
        own_out[rows, :] = held_ref[0, rows, :]
        own_out[32 + time * 8 : 40 + time * 8, :] = held_ref[1, rows, :] + held_ref[2, rows, :] * total
    for kind in range(2):
        for half in range(2):
            for y in range(4):
                rows_out[(kind * 2 + half) * 4 : (kind * 2 + half) * 4 + 4, y * 128 : y * 128 + 128] = own_out[
                    pl.ds(kind * 32 + half * 4 + y, 4, stride=8), :
                ]
    ordered = split_dot(rows_out[0:16, :], perm_ref[...], 3, transposed=True)
    for target in range(32):
        spot, half = target // 2, target % 2
        lanes = slice(spot * 32, spot * 32 + 32)
        out_ref[target] = jnp.zeros((8, 128), F32)
        out_ref[target, 0:4, 0:32] = ordered[half * 4 : half * 4 + 4, lanes]
        out_ref[target, 0:4, 32:64] = ordered[8 + half * 4 : 12 + half * 4, lanes]


def unpack_kernel(in_ref, flowed_ref, grad_ref, g1_ref, g2_ref, g3_ref, b1_ref, b2_ref, b3_ref, window, extra, turned_x):
    for source in range(32):
        window[4 * source : 4 * source + 4, :] = in_ref[source, 8:12, :]
    turned = window[0:128, :].T
    flowed_ref[...] = turned[0:32]
    grad_ref[...] = turned[32:64]

    def group(number):
        return jnp.concatenate([in_ref[2 * number, 0:8, :], in_ref[2 * number + 1, 0:8, :]], axis=0)

    for number in range(11):
        block = group(number)
        for slot in range(min(8, 81 - number * 8)):
            g2_ref[number * 8 + slot] = block[:, slot * 16 : slot * 16 + 16]
    for number in range(4):
        extra[number * 16 : number * 16 + 16, :] = group(11 + number)
    extra[64:128, :] = jnp.zeros((64, 128), F32)
    turned_x[0:128, :] = extra[...].T
    for et in range(3):
        lanes = slice(et * 16, et * 16 + 16)
        for ey in range(3):
            for ex in range(3):
                for ez in range(3):
                    off = ((ex * 3 + ey) * 3 + ez) * 3
                    row = ey * 24 + (2 - ex) * 8
                    if ez < 2:
                        g1_ref[off + et] = turned_x[row + 6 + ez : row + 7 + ez, lanes]
                    else:
                        g1_ref[off + et] = turned_x[row + et : row + et + 1, 48:64]
                    row = (2 - ey) * 24 + ex * 8 + ez
                    g3_ref[off + 2 - et, 0:1, :] = turned_x[row : row + 1, lanes]
                    g3_ref[off + 2 - et, 1:2, :] = turned_x[row + 3 : row + 4, lanes]
    sums = in_ref[30, 0:8, :]
    lane = lax.broadcasted_iota(jnp.int32, (1, 128), 1)
    total = jnp.sum(sums, axis=1, keepdims=True)
    b3_ref[...] = jnp.where(lane == 0, total[2:3], total[3:4])[:, 0:2]
    for step in (64, 32, 16):
        sums = sums + pltpu.roll(sums, step, 1)
    b1_ref[...] = sums[0:1, 0:16]
    b2_ref[...] = sums[1:2, 0:16]


def ring(count, step):
    return [(i, (i + step) % count) for i in range(count)]


def shape(dims, dtype=F32):
    return jax.ShapeDtypeStruct(dims, dtype)


def run_weights(kernel_one, bias_one, kernel_two, bias_two, kernel_three, bias_three):
    return pl.pallas_call(
        weights_kernel,
        out_shape=[
            shape((384, 128), BF16),
            shape((768, 128), BF16),
            shape((4608, 256), BF16),
            shape((4608, 256), BF16),
            shape((1152, 128), BF16),
            shape((1152, 128), BF16),
            shape((8, 128)),
            shape((512, 512), BF16),
        ],
        in_specs=[VMEM_SPEC] * 6,
        out_specs=[VMEM_SPEC] * 8,
        scratch_shapes=[
            pltpu.VMEM((96, 128), F32),
            pltpu.VMEM((1296, 128), F32),
            pltpu.VMEM((176, 128), F32),
        ],
        compiler_params=pltpu.CompilerParams(vmem_limit_bytes=12 * 2**20),
        cost_estimate=pl.CostEstimate(flops=10**6, bytes_accessed=8 * 10**6, transcendentals=0),
        name="weights",
    )(
        kernel_one[:, 0].transpose(1, 2, 3, 4, 0).reshape(81, 16),
        kernel_two.transpose(2, 3, 4, 5, 0, 1).reshape(1296, 16),
        kernel_three.transpose(2, 3, 4, 5, 0, 1).reshape(162, 16),
        bias_one.reshape(1, 16),
        bias_two.reshape(1, 16),
        bias_three.reshape(1, 2),
    )


def run_main(*operands, name="flow"):
    return pl.pallas_call(
        main_kernel,
        out_shape=[
            shape((32, 8, 128)),
            shape((6, 5, 2, 16, 384), BF16),
            shape((3, 32, 128)),
        ],
        in_specs=[VMEM_SPEC] * 10,
        out_specs=[VMEM_SPEC] * 3,
        scratch_shapes=[
            pltpu.VMEM((18, 24, 512), F32),
            pltpu.VMEM((576, 128), F32),
            pltpu.VMEM((576, 128), F32),
            pltpu.VMEM((576, 128), F32),
            pltpu.VMEM((432, 128), F32),
            pltpu.VMEM((18, 20, 16, 128), BF16),
            pltpu.VMEM((16, 10, 2, 16, 384), BF16),
            pltpu.VMEM((14, 9, 2, 16, 384), BF16),
            pltpu.VMEM((12, 16, 128), F32),
            pltpu.VMEM((12, 16, 128), F32),
            pltpu.VMEM((12, 16, 128), F32),
            pltpu.VMEM((10, 16, 128), F32),
            pltpu.VMEM((10, 16, 128), F32),
            pltpu.VMEM((10, 16, 128), F32),
            pltpu.VMEM((10, 12, 16, 256), BF16),
            pltpu.VMEM((8, 6, 2, 16, 384), BF16),
        ],
        compiler_params=pltpu.CompilerParams(vmem_limit_bytes=28 * 2**20),
        cost_estimate=pl.CostEstimate(flops=2 * 10**10, bytes_accessed=8 * 10**6, transcendentals=10**6),
        name=name,
    )(*operands)


def main_shapes():
    return [
        shape((32, 16, 128), BF16), shape((32, 16, 128), BF16), shape((32, 16, 128), BF16), shape((512, 512), BF16), shape((384, 128), BF16), shape((768, 128), BF16),
        shape((4608, 256), BF16), shape((4608, 256), BF16), shape((1152, 128), BF16), shape((8, 128)),
    ]


def local(field, parity_mask, kernel_one, bias_one, kernel_two, bias_two, kernel_three, bias_three):
    packed = pl.pallas_call(
        pack_kernel,
        out_shape=shape((32, 16, 128), BF16),
        in_specs=[VMEM_SPEC] * 2,
        out_specs=VMEM_SPEC,
        scratch_shapes=[pltpu.VMEM((3, 144, 128), F32)],
        name="pack",
    )(field.reshape(32, 128), parity_mask.reshape(32, 128))
    own = lax.all_to_all(packed, GROUP, 0, 0)
    low = lax.ppermute(own, "gyh", ring(8, 1))
    high = lax.ppermute(own, "gyh", ring(8, -1))
    w1, w3t, w2, w2t, w3, w1t, bias, perm = run_weights(
        kernel_one, bias_one, kernel_two, bias_two, kernel_three, bias_three
    )
    shares, cot1, held = run_main(low, own, high, perm, w1, w3t, w2, w2t, w3, bias)
    shares = lax.all_to_all(shares, GROUP, 0, 0)
    outputs = pl.pallas_call(
        input_grad_kernel,
        out_shape=shape((32, 8, 128)),
        in_specs=[VMEM_SPEC] * 4,
        out_specs=VMEM_SPEC,
        scratch_shapes=[
            pltpu.VMEM((96, 128), F32),
            pltpu.VMEM((24, 512), F32),
        ],
        compiler_params=pltpu.CompilerParams(vmem_limit_bytes=8 * 2**20),
        cost_estimate=pl.CostEstimate(flops=5 * 10**8, bytes_accessed=3 * 10**6, transcendentals=0),
        name="input_grad",
    )(cot1, held, w1t, perm)
    share = jnp.broadcast_to(jnp.sum(shares, axis=0)[None], (8, 8, 128))
    share = lax.all_to_all(share, "gyh", 0, 0)
    share = jnp.sum(share, axis=0) * (1.0 / VOLUME)
    last = jnp.concatenate([jnp.broadcast_to(share[None], (32, 8, 128)), outputs], axis=1)
    last = lax.all_to_all(last, GROUP, 0, 0)
    flowed, field_grad, g1, g2, g3, b1, b2, b3 = pl.pallas_call(
        unpack_kernel,
        out_shape=[
            shape((32, 128)), shape((32, 128)), shape((81, 1, 16)), shape((81, 16, 16)), shape((81, 2, 16)),
            shape((1, 16)), shape((1, 16)), shape((1, 2)),
        ],
        in_specs=[VMEM_SPEC],
        out_specs=[VMEM_SPEC] * 8,
        scratch_shapes=[pltpu.VMEM((136, 128), F32), pltpu.VMEM((128, 128), F32), pltpu.VMEM((136, 128), F32)],
        name="unpack",
    )(last)
    return (
        flowed.reshape(2, 4, 4, 128),
        field_grad.reshape(2, 4, 4, 128),
        g1.reshape(3, 3, 3, 3, 1, 16).transpose(5, 4, 0, 1, 2, 3),
        b1.reshape(16),
        g2.reshape(3, 3, 3, 3, 16, 16).transpose(4, 5, 0, 1, 2, 3),
        b2.reshape(16),
        g3.reshape(3, 3, 3, 3, 2, 16).transpose(4, 5, 0, 1, 2, 3),
        b3.reshape(2),
    )


def solution(mesh):
    split = Mesh(mesh.devices.reshape(8, 8, 2, 2), ("gx", "gyh", "gyl", "gz"))
    block = P("gx", ("gyh", "gyl"), "gz", None)
    return jax.shard_map(
        local,
        mesh=split,
        in_specs=(block, block, P(), P(), P(), P(), P(), P()),
        out_specs=(block, block, P(), P(), P(), P(), P(), P()),
        check_vma=False,
    )
```
